256 devices in a mesh: group: 4 (over x), within: 64 (over z, y, core).
Axes of the slice: x: 4, y: 4, z: 8, core: 2. Of those that a mesh axis runs over, the one named last changes fastest.
Arguments:
- coords: float32 [1048576, 64], P(('group', 'within')), may hold values from -6 to 6
- perm: int32 [1048576], P(('group', 'within')), may hold values from 0 to 4095, as said below
- inv_scale: float32 [64], replicated, may hold values from 0.08 to 0.4
- noise: float32 [1], replicated, may hold values from 0.1 to 1
- leaf_basis: float32 [1048576, 64], P(('group', 'within')), may hold values from -0.25 to 0.25
- pair_transfer: float32 [2048, 64, 128], P(('group', 'within')), may hold values from -0.5 to 0.5
- coupling: float32 [2048, 64, 64], P(('group', 'within')), may hold values from -0.75 to 0.75
- solution: float32 [1048576, 64], P(('group', 'within')), may hold values from -6 to 6
- residual: float32 [1048576, 64], P(('group', 'within')), may hold values from -6 to 6
- direction: float32 [1048576, 64], P(('group', 'within')), may hold values from -6 to 6
Outputs:
- new_solution: float32 [1048576, 64], P(('group', 'within'))
- new_residual: float32 [1048576, 64], P(('group', 'within'))
- new_direction: float32 [1048576, 64], P(('group', 'within'))
The draws below stay inside these ranges and needn't reach their ends.
Inputs may be any that keep to these rules, and one draw needn't show every extreme that they name: `perm`: each aligned block of 4096 entries holds every number from 0 to 4095 exactly once.
All inputs are finite; a program needn't handle non-finite values.
Results may differ from the reference program's by a relative error of at most 0.00012.
Values sent between devices are 32-bit elements; how exact they have to be, the bound alone decides.
A program may use at most 128 MiB of HBM per device.

```python
import math
import jax
import jax.numpy as jnp
from jax import lax

DIM = 64
LEAF = 512
RANK = 64
NRHS = 64
LEAF_DEV = 8
N = 1048576
NLEAF = 2048


def draw_perm(key, part):
    key = jax.random.fold_in(key, 11)
    block_rows = LEAF * LEAF_DEV
    blocks = N // block_rows
    keys = jax.random.split(key, blocks)
    local = jax.vmap(lambda one: jax.random.permutation(one, block_rows))(keys)
    return local.astype(jnp.int32).reshape(-1).astype(jnp.int32)


def levels(own_key, shape, pieces, low, high):
    factor_of, own = 1.0, jax.random.fold_in(own_key, 6)
    for position, shards_of in pieces:
        steps = jnp.exp(jax.random.uniform(jax.random.fold_in(own, position), (shards_of,), jnp.float32, low / len(pieces), high / len(pieces)))
        factor_of = factor_of * jnp.repeat(steps, shape[position] // shards_of).reshape([-1 if axis == position else 1 for axis in range(len(shape))])
    return factor_of


def normal_values(key, extent, deviation, most, cuts=(), kind=jnp.bfloat16):
    values = deviation * jax.random.normal(key, extent, jnp.float32)
    if cuts:
        values = values * levels(key, extent, cuts, -0.22, 0.18)
    return jnp.clip(values, -most, most).astype(kind)


def setup_inputs(seed: int = 0) -> dict:
    seeds = jax.random.split(jax.random.key(seed), 11)
    return {
        "coords": normal_values(seeds[0], (N, DIM), 1.0, 6.0, ((0, 256),), jnp.float32),
        "perm": draw_perm(jax.random.fold_in(seeds[10], 71), 0),
        "inv_scale": jnp.clip(jnp.exp(jax.random.uniform(seeds[2], (DIM,), jnp.float32, math.log(0.08), math.log(0.4))), 0.08, 0.4),
        "noise": jnp.clip(jnp.exp(jax.random.uniform(seeds[3], (1,), jnp.float32, math.log(0.1), math.log(1.0))), 0.1, 1.0),
        "leaf_basis": normal_values(seeds[4], (N, RANK), LEAF ** -0.5, 0.25, ((0, 256),), jnp.float32),
        "pair_transfer": normal_values(seeds[5], (NLEAF, RANK, 2 * RANK), (2 * RANK) ** -0.5, 0.5, ((0, 256),), jnp.float32),
        "coupling": normal_values(seeds[6], (NLEAF, RANK, RANK), RANK ** -0.5, 0.75, ((0, 256),), jnp.float32),
        "solution": normal_values(seeds[7], (N, NRHS), 1.0, 6.0, ((0, 256),), jnp.float32),
        "residual": normal_values(seeds[8], (N, NRHS), 1.0, 6.0, ((0, 256),), jnp.float32),
        "direction": normal_values(seeds[9], (N, NRHS), 1.0, 6.0, ((0, 256),), jnp.float32),
    }


HIGH = lax.Precision.HIGHEST
ROOT_FIVE = math.sqrt(5.0)

def matern_block(scaled):
    squares = lax.optimization_barrier(jnp.sum(scaled * scaled, axis=1))
    inner = jnp.dot(scaled, scaled.T, precision=HIGH)
    dist_sq = jnp.maximum(squares[:, None] + squares[None, :] - 2.0 * inner, 0.0)
    dist = jnp.sqrt(dist_sq)
    return (1.0 + ROOT_FIVE * dist + 5.0 / 3.0 * dist_sq) * jnp.exp(-ROOT_FIVE * dist)

def leaf_product(item):
    return jnp.dot(matern_block(item[0]), item[1], precision=HIGH)

def raise_pair(transfer, left, right):
    width = left.shape[1]
    upper = jnp.einsum('kab,kan->kbn', transfer[:, :, :width], left, precision=HIGH)
    return upper + jnp.einsum('kab,kan->kbn', transfer[:, :, width:], right, precision=HIGH)

def lower_pair(transfer, couple, left, right, parent):
    width = left.shape[1]
    f_left = jnp.einsum('kab,kbn->kan', couple, right, precision=HIGH) + jnp.einsum('kab,kbn->kan', transfer[:, :, :width], parent, precision=HIGH)
    f_right = jnp.einsum('kba,kbn->kan', couple, left, precision=HIGH) + jnp.einsum('kab,kbn->kan', transfer[:, :, width:], parent, precision=HIGH)
    return jnp.stack([f_left, f_right], axis=1).reshape(-1, width, left.shape[2])

def reference(coords, perm, inv_scale, noise, leaf_basis, pair_transfer, coupling, solution, residual, direction):
    nleaves = N // LEAF
    heights = nleaves.bit_length() - 1
    block_rows = LEAF * LEAF_DEV
    starts = (jnp.arange(N, dtype=jnp.int32) // block_rows * block_rows).astype(jnp.int32)
    points = (coords[(perm + starts).astype(jnp.int32)] * inv_scale).reshape(nleaves, LEAF, DIM)
    vectors = direction.reshape(nleaves, LEAF, NRHS)
    dense = lax.map(leaf_product, (points, vectors))
    basis = leaf_basis.reshape(nleaves, LEAF, RANK)
    coeff = jnp.einsum('lpr,lpn->lrn', basis, vectors, precision=HIGH)
    stacked = []
    for height in range(1, heights + 1):
        chosen = pair_transfer[2 ** (height - 1) - 1::2 ** height]
        left, right = (coeff[0::2], coeff[1::2])
        stacked.append((left, right))
        coeff = raise_pair(chosen, left, right)
    far = jnp.zeros((1, RANK, NRHS), jnp.float32)
    for height in range(heights, 0, -1):
        chosen = pair_transfer[2 ** (height - 1) - 1::2 ** height]
        couple = coupling[2 ** (height - 1) - 1::2 ** height]
        left, right = stacked[height - 1]
        far = lower_pair(chosen, couple, left, right, far)
    image = dense + noise[0] * vectors + jnp.einsum('lpr,lrn->lpn', basis, far, precision=HIGH)
    image = image.reshape(N, NRHS)
    old_rr = lax.optimization_barrier(jnp.sum(residual * residual, axis=0))
    curve = lax.optimization_barrier(jnp.sum(direction * image, axis=0))
    alpha = old_rr / curve
    new_solution = solution + alpha * direction
    new_residual = residual - alpha * image
    new_rr = lax.optimization_barrier(jnp.sum(new_residual * new_residual, axis=0))
    new_direction = new_residual + new_rr / old_rr * direction
    return (new_solution, new_residual, new_direction)
```

```python
import functools
import math

import jax
import jax.numpy as jnp
from jax import lax
from jax.experimental import pallas as pl
from jax.experimental.pallas import tpu as pltpu
from jax.sharding import PartitionSpec as P

LEAF = 512
RANK = 64
COLS = 64
ROWS = 4096
NLEAF = 8
ROOT_FIVE = math.sqrt(5.0)
MESH = pl.DeviceIdType.MESH
F32 = jnp.float32
BF16 = jnp.bfloat16
NT = (((1,), (1,)), ((), ()))
NN = (((1,), (0,)), ((), ()))


def split(a):
    high = a.astype(BF16)
    return high, (a - high.astype(F32)).astype(BF16)


def mxu(a, b, dims=NN):
    return lax.dot_general(a, b, dims, preferred_element_type=F32)


def product(a, b, dims=NN):
    ah, al = split(a)
    bh, bl = split(b)
    return mxu(ah, bh, dims) + (mxu(ah, bl, dims) + mxu(al, bh, dims))


def pack(c):
    return jnp.concatenate([c[0:32], c[32:64]], axis=1)


def unpack(p):
    return jnp.concatenate([p[:, 0:64], p[:, 64:128]], axis=0)


def raise_pair(transfer, left, right):
    return product(
        jnp.concatenate([left, right], axis=1),
        jnp.concatenate([transfer[:, 0:64], transfer[:, 64:128]], axis=0),
    )


def lower_left(transfer, couple, right, parent):
    return product(
        jnp.concatenate([right, parent], axis=1),
        jnp.concatenate([couple, transfer[:, 0:64]], axis=1),
        NT,
    )


def lower_right(transfer, couple, left, parent):
    return product(
        jnp.concatenate([left, parent], axis=1),
        jnp.concatenate([couple.T, transfer[:, 64:128]], axis=1),
        NT,
    )


def lower_side(is_left, transfer, couple, sibling, parent):
    side = jnp.where(is_left, transfer[:, 0:64], transfer[:, 64:128])
    across = jnp.where(is_left, couple, couple.T)
    if parent is None:
        return product(sibling, across, NT)
    return product(
        jnp.concatenate([sibling, parent], axis=1),
        jnp.concatenate([across, side], axis=1),
        NT,
    )


def kernel(
    coords, perm, scale, noise, basis, transfer, coupling, sol, res, direc,
    out_sol, out_res, out_dir,
    x_in, x_rows, x_perm, b_in, t_in, k_in, s_in, r_in, d_in, image,
    d_split, b_split, leaf_c, leaf_f,
    mat_a, mat_z, mat_x, c_a, c_z, c_x, f_top, pair_c, reduce,
    in_sem, out_sem, send_sem, rm_a, rm_z, rm_x, rc_a, rc_z, rc_x, r_f, r_red,
):
    group = lax.axis_index("group")
    within = lax.axis_index("within")
    slab = group
    line = lax.div(within, 8)
    spot = lax.rem(within, 8)
    leader = spot == 7
    top_line = line == 7

    def in_plane(q):
        return (group, line * 8 + q)

    def in_line(q):
        return (group, q * 8 + spot)

    def in_slab(q):
        return (q, within)

    inputs = [
        (transfer, t_in), (coupling, k_in), (direc, d_in), (basis, b_in),
        (coords, x_in), (res, r_in), (sol, s_in),
    ]
    loads = [
        pltpu.make_async_copy(src, dst, in_sem.at[i]) for i, (src, dst) in enumerate(inputs)
    ]
    for load in loads:
        load.start()

    barrier = pltpu.get_barrier_semaphore()

    def greet(device):
        pl.semaphore_signal(barrier, inc=1, device_id=device, device_id_type=MESH)

    for p in range(1, 8):
        greet(in_plane(lax.rem(spot + p, 8)))
        greet(in_line(lax.rem(line + p, 8)))
    for p in range(1, 4):
        greet(in_slab(lax.rem(slab + p, 4)))

    @pl.when(jnp.logical_and(leader, jnp.logical_not(top_line)))
    def _():
        for q in range(3):
            @pl.when(slab != q)
            def _():
                greet((q, 63))

    sends = []

    def remote(src, dst, recv, device):
        index = len(sends)
        copy = pltpu.make_async_remote_copy(
            src_ref=src, dst_ref=dst, send_sem=send_sem.at[index], recv_sem=recv,
            device_id=device, device_id_type=MESH,
        )
        sends.append(copy)
        return copy

    def arrived(dst, recv):
        pltpu.make_async_remote_copy(
            src_ref=dst, dst_ref=dst, send_sem=send_sem.at[0], recv_sem=recv,
            device_id=in_plane(lax.rem(spot + 1, 8)), device_id_type=MESH,
        ).wait_recv()

    loads[0].wait()
    loads[1].wait()
    own = jnp.concatenate([t_in[7], pack(k_in[7])], axis=0)

    @pl.when(jnp.logical_not(leader))
    def _():
        mat_a[spot] = own

    @pl.when(jnp.logical_and(leader, jnp.logical_not(top_line)))
    def _():
        mat_z[line] = own

    @pl.when(jnp.logical_and(leader, top_line))
    def _():
        mat_x[slab] = own

    owner = jnp.logical_and(jnp.logical_and(leader, top_line), slab < 3)
    pl.semaphore_wait(barrier, jnp.where(owner, 38, 17))

    send_a = [
        remote(mat_a.at[spot], mat_a.at[spot], rm_a.at[spot], in_plane(lax.rem(spot + p, 8)))
        for p in range(1, 8)
    ]
    send_z = [
        remote(mat_z.at[line], mat_z.at[line], rm_z.at[line], in_line(lax.rem(line + p, 8)))
        for p in range(1, 8)
    ]
    first_x = len(sends)
    flat = slab * 8 + line

    def send_top(p):
        q = lax.rem(flat + p, 32)
        return pltpu.make_async_remote_copy(
            src_ref=mat_x.at[slab], dst_ref=mat_x.at[slab], send_sem=send_sem.at[first_x + p - 1],
            recv_sem=rm_x.at[slab], device_id=(lax.div(q, 8), lax.rem(q, 8) * 8 + 7), device_id_type=MESH,
        )
    sends.extend([None] * 31)

    @pl.when(jnp.logical_not(leader))
    def _():
        for copy in send_a:
            copy.start()

    @pl.when(jnp.logical_and(leader, jnp.logical_not(top_line)))
    def _():
        for copy in send_z:
            copy.start()

    @pl.when(owner)
    def _():
        @pl.loop(1, 32)
        def _(p):
            send_top(p).start()

    loads[2].wait()
    loads[3].wait()

    @pl.loop(0, NLEAF)
    def _(leaf):
        at = pl.multiple_of(leaf * LEAF, LEAF)
        dh, dl = split(d_in[:, pl.ds(at, LEAF)])
        bh, bl = split(b_in[:, pl.ds(at, LEAF)])
        both_d = jnp.concatenate([dh, dl], axis=0)
        both_b = jnp.concatenate([bh, bl], axis=0)
        d_split[:, pl.ds(at, LEAF)] = both_d
        b_split[:, pl.ds(at, LEAF)] = both_b
        prod = mxu(both_d, both_b, NT)
        leaf_c[leaf] = (prod[0:64, 0:64] + prod[64:128, 64:128]) + (prod[0:64, 64:128] + prod[64:128, 0:64])

    for k in range(4):
        leaf_c[8 + k] = raise_pair(t_in[2 * k], leaf_c[2 * k], leaf_c[2 * k + 1])
    for k in range(2):
        leaf_c[12 + k] = raise_pair(t_in[4 * k + 1], leaf_c[8 + 2 * k], leaf_c[9 + 2 * k])
    c_a[spot] = pack(raise_pair(t_in[3], leaf_c[12], leaf_c[13]))
    send_ca = [
        remote(c_a.at[spot], c_a.at[spot], rc_a.at[spot], in_plane(lax.rem(spot + p, 8)))
        for p in range(1, 8)
    ]
    for copy in send_ca:
        copy.start()

    loads[4].wait()

    @pl.loop(0, ROWS // 128)
    def _(i):
        at = pl.multiple_of(i * 128, 128)
        x_rows[pl.ds(at, 128), 0:64] = x_in[:, pl.ds(at, 128)].T * (ROOT_FIVE * scale[...])

    def dense(first, last):
        @pl.loop(first, last)
        def _(leaf):
            at = pl.multiple_of(leaf * LEAF, LEAF)

            @pl.loop(0, LEAF // 32)
            def _(i):
                base = pl.multiple_of(i * 32, 32)
                for j in range(32):
                    x_perm[pl.ds(base + j, 1), :] = x_rows[pl.ds(perm[at + base + j], 1), :]

            xh, xl = split(x_perm[:, 0:64])
            near = xh.astype(F32) + xl.astype(F32)
            square = jnp.sum(near * near, axis=1, keepdims=True)
            square_row = jnp.broadcast_to(square, (LEAF, 128)).T[0:1]
            one = jnp.concatenate([xh, xh, xl, xl], axis=1)
            two = jnp.concatenate([xh, xl, xh, xl], axis=1)
            vectors = d_split[:, pl.ds(at, LEAF)].T
            for c in range(0, LEAF, 128):
                inner = mxu(one[c : c + 128], two, NT)
                dist_sq = jnp.maximum((square[c : c + 128] + square_row) - 2.0 * inner, 1e-30)
                dist = dist_sq * lax.rsqrt(dist_sq)
                value = (1.0 + dist + dist_sq * (1.0 / 3.0)) * jnp.exp(-dist)
                vh, vl = split(value)
                got = mxu(vh, vectors) + mxu(vl, vectors)
                image[:, pl.ds(at + c, 128)] = (got[:, 0:64] + got[:, 64:128]).T

    def mats(ref):
        return ref[0:64, :], unpack(ref[64:96, :])

    dense(0, 3)

    for p in range(1, 8):
        q = lax.rem(spot + p, 8)
        arrived(c_a.at[q], rc_a.at[q])

        @pl.when(q != 7)
        def _():
            arrived(mat_a.at[q], rm_a.at[q])
    for k in range(4):
        pair_c[k] = raise_pair(mat_a[2 * k, 0:64, :], unpack(c_a[2 * k]), unpack(c_a[2 * k + 1]))
    for k in range(2):
        pair_c[4 + k] = raise_pair(mat_a[4 * k + 1, 0:64, :], pair_c[2 * k], pair_c[2 * k + 1])

    send_cz = [
        remote(c_z.at[line], c_z.at[line], rc_z.at[line], in_line(lax.rem(line + p, 8)))
        for p in range(1, 8)
    ]
    send_cx = [
        remote(c_x.at[slab], c_x.at[slab], rc_x.at[slab], in_slab(lax.rem(slab + p, 4)))
        for p in range(1, 4)
    ]
    send_f = [
        remote(f_top, f_top, r_f, in_plane(lax.rem(spot + p, 8)))
        for p in range(1, 8)
    ]

    @pl.when(leader)
    def _():
        c_z[line] = pack(raise_pair(mat_a[3, 0:64, :], pair_c[4], pair_c[5]))
        for copy in send_cz:
            copy.start()

    dense(3, 5)

    @pl.when(leader)
    def _():
        for p in range(1, 8):
            q = lax.rem(line + p, 8)
            arrived(c_z.at[q], rc_z.at[q])

            @pl.when(q != 7)
            def _():
                arrived(mat_z.at[q], rm_z.at[q])
        for k in range(4):
            pair_c[6 + k] = raise_pair(mat_z[2 * k, 0:64, :], unpack(c_z[2 * k]), unpack(c_z[2 * k + 1]))
        for k in range(2):
            pair_c[10 + k] = raise_pair(mat_z[4 * k + 1, 0:64, :], pair_c[6 + 2 * k], pair_c[7 + 2 * k])
        c_x[slab] = pack(raise_pair(mat_z[3, 0:64, :], pair_c[10], pair_c[11]))
        for copy in send_cx:
            copy.start()

    dense(5, 7)

    @pl.when(leader)
    def _():
        for p in range(1, 4):
            q = lax.rem(slab + p, 4)
            arrived(c_x.at[q], rc_x.at[q])
        for q in range(3):
            @pl.when(jnp.logical_or(slab != q, jnp.logical_not(top_line)))
            def _():
                arrived(mat_x.at[q], rm_x.at[q])
        for k in range(2):
            pair_c[12 + k] = raise_pair(mat_x[2 * k, 0:64, :], unpack(c_x[2 * k]), unpack(c_x[2 * k + 1]))
        half = lax.div(slab, 2)
        t, b = mats(mat_x.at[1])
        far = lower_side(half == 0, t, b, pair_c[13 - half], None)
        t, b = mats(mat_x.at[half * 2])
        side = lax.rem(slab, 2)
        far = lower_side(side == 0, t, b, unpack(c_x[half * 2 + 1 - side]), far)
        half = lax.div(line, 4)
        t, b = mats(mat_z.at[3])
        far = lower_side(half == 0, t, b, pair_c[11 - half], far)
        quarter = lax.div(line, 2)
        side = lax.rem(quarter, 2)
        t, b = mats(mat_z.at[half * 4 + 1])
        far = lower_side(side == 0, t, b, pair_c[6 + half * 2 + 1 - side], far)
        side = lax.rem(line, 2)
        t, b = mats(mat_z.at[quarter * 2])
        far = lower_side(side == 0, t, b, unpack(c_z[quarter * 2 + 1 - side]), far)
        f_top[...] = pack(far)
        for copy in send_f:
            copy.start()

    dense(7, 8)

    @pl.when(jnp.logical_not(leader))
    def _():
        arrived(f_top, r_f)
    far = unpack(f_top[...])
    half = lax.div(spot, 4)
    t, b = mats(mat_a.at[3])
    far = lower_side(half == 0, t, b, pair_c[5 - half], far)
    quarter = lax.div(spot, 2)
    side = lax.rem(quarter, 2)
    t, b = mats(mat_a.at[half * 4 + 1])
    far = lower_side(side == 0, t, b, pair_c[half * 2 + 1 - side], far)
    side = lax.rem(spot, 2)
    t, b = mats(mat_a.at[quarter * 2])
    far = lower_side(side == 0, t, b, unpack(c_a[quarter * 2 + 1 - side]), far)
    near = [far]
    for height, first in ((3, 12), (2, 8), (1, 0)):
        below = []
        for k, parent in enumerate(near):
            node = k * 2**height + 2 ** (height - 1) - 1
            left, right = leaf_c[first + 2 * k], leaf_c[first + 2 * k + 1]
            below.append(lower_left(t_in[node], k_in[node], right, parent))
            below.append(lower_right(t_in[node], k_in[node], left, parent))
        near = below
    for k in range(NLEAF):
        fh, fl = split(near[k])
        leaf_f[k] = jnp.concatenate(
            [jnp.concatenate([fh, fh], axis=1), jnp.concatenate([fl, fl], axis=1)], axis=0
        )

    loads[5].wait()
    loads[6].wait()
    shift = noise[0]
    zero = jnp.zeros((COLS, 128), F32)

    def add_leaf(leaf, sums):
        at = pl.multiple_of(leaf * LEAF, LEAF)
        far = mxu(leaf_f[leaf], b_split[:, pl.ds(at, LEAF)])
        d = d_in[:, pl.ds(at, LEAF)]
        r = r_in[:, pl.ds(at, LEAF)]
        q = image[:, pl.ds(at, LEAF)] + shift * d + (far[0:64] + far[64:128])
        image[:, pl.ds(at, LEAF)] = q
        terms = (r * r, d * q, r * q, q * q)
        return tuple(
            total + ((term[:, 0:128] + term[:, 128:256]) + (term[:, 256:384] + term[:, 384:512]))
            for total, term in zip(sums, terms)
        )

    sums = lax.fori_loop(0, NLEAF, add_leaf, (zero, zero, zero, zero))
    lane = lax.broadcasted_iota(jnp.int32, (COLS, 128), 1)
    table = zero
    for i, total in enumerate(sums):
        table = jnp.where(lane == i, jnp.sum(total, axis=1, keepdims=True), table)
    value = table.T[0:8, :]

    first = 0
    send_red = []
    for size, place, device in ((8, spot, in_plane), (8, line, in_line), (4, slab, in_slab)):
        reduce[first + place, :, 0:64] = value
        copies = []
        for p in range(1, size):
            q = lax.rem(place + p, size)
            copies.append(
                remote(reduce.at[first + place], reduce.at[first + place], r_red.at[first + place], device(q))
            )
        for copy in copies:
            copy.start()
        send_red.extend(copies)
        for p in range(1, size):
            q = lax.rem(place + p, size)
            arrived(reduce.at[first + q], r_red.at[first + q])
        value = reduce[first, :, 0:64]
        for q in range(1, size):
            value = value + reduce[first + q, :, 0:64]
        first += size

    old, curve, cross, own_square = value[0:1], value[1:2], value[2:3], value[3:4]
    alpha = old / curve
    new = old - 2.0 * alpha * cross + alpha * alpha * own_square
    ratio = new / old
    alpha = jnp.broadcast_to(alpha, (128, COLS)).T
    ratio = jnp.broadcast_to(ratio, (128, COLS)).T
    alpha = jnp.concatenate([alpha] * 4, axis=1)
    ratio = jnp.concatenate([ratio] * 4, axis=1)

    def stores(leaf):
        at = pl.multiple_of(leaf * LEAF, LEAF)
        return [
            pltpu.make_async_copy(src.at[:, pl.ds(at, LEAF)], dst.at[:, pl.ds(at, LEAF)], out_sem.at[i, leaf])
            for i, (src, dst) in enumerate(((s_in, out_sol), (r_in, out_res), (image, out_dir)))
        ]

    @pl.loop(0, NLEAF)
    def _(leaf):
        at = pl.multiple_of(leaf * LEAF, LEAF)
        d = d_in[:, pl.ds(at, LEAF)]
        r = r_in[:, pl.ds(at, LEAF)] - alpha * image[:, pl.ds(at, LEAF)]
        s_in[:, pl.ds(at, LEAF)] = s_in[:, pl.ds(at, LEAF)] + alpha * d
        r_in[:, pl.ds(at, LEAF)] = r
        image[:, pl.ds(at, LEAF)] = r + ratio * d
        for copy in stores(leaf):
            copy.start()

    for copy in send_ca + send_red:
        copy.wait_send()

    @pl.when(jnp.logical_not(leader))
    def _():
        for copy in send_a:
            copy.wait_send()

    @pl.when(leader)
    def _():
        for copy in send_cz + send_cx + send_f:
            copy.wait_send()

    @pl.when(jnp.logical_and(leader, jnp.logical_not(top_line)))
    def _():
        for copy in send_z:
            copy.wait_send()

    @pl.when(owner)
    def _():
        @pl.loop(1, 32)
        def _(p):
            send_top(p).wait_send()

    @pl.loop(0, NLEAF)
    def _(leaf):
        for copy in stores(leaf):
            copy.wait()


def on_device(
    coords, perm, inv_scale, noise, leaf_basis, pair_transfer, coupling, solution, residual, direction
):
    hbm = pl.BlockSpec(memory_space=pl.ANY)
    smem = pl.BlockSpec(memory_space=pltpu.SMEM)
    vmem = pl.BlockSpec(memory_space=pltpu.VMEM)
    wide = jax.ShapeDtypeStruct((COLS, ROWS), F32)
    dma = pltpu.SemaphoreType.DMA
    outs = pl.pallas_call(
        kernel,
        out_shape=(wide, wide, wide),
        in_specs=[hbm, smem, vmem, smem, hbm, hbm, hbm, hbm, hbm, hbm],
        out_specs=(hbm, hbm, hbm),
        scratch_shapes=[
            pltpu.VMEM((64, ROWS), F32),
            pltpu.VMEM((ROWS, 128), F32),
            pltpu.VMEM((LEAF, 128), F32),
            pltpu.VMEM((64, ROWS), F32),
            pltpu.VMEM((8, 64, 128), F32),
            pltpu.VMEM((8, 64, 64), F32),
            pltpu.VMEM((64, ROWS), F32),
            pltpu.VMEM((64, ROWS), F32),
            pltpu.VMEM((64, ROWS), F32),
            pltpu.VMEM((64, ROWS), F32),
            pltpu.VMEM((128, ROWS), BF16),
            pltpu.VMEM((128, ROWS), BF16),
            pltpu.VMEM((14, 64, 64), F32),
            pltpu.VMEM((8, 128, 128), BF16),
            pltpu.VMEM((8, 96, 128), F32),
            pltpu.VMEM((8, 96, 128), F32),
            pltpu.VMEM((4, 96, 128), F32),
            pltpu.VMEM((8, 32, 128), F32),
            pltpu.VMEM((8, 32, 128), F32),
            pltpu.VMEM((4, 32, 128), F32),
            pltpu.VMEM((32, 128), F32),
            pltpu.VMEM((14, 64, 64), F32),
            pltpu.VMEM((20, 8, 128), F32),
            dma((7,)),
            dma((3, NLEAF)),
            dma((96,)),
            dma((8,)),
            dma((8,)),
            dma((4,)),
            dma((8,)),
            dma((8,)),
            dma((4,)),
            dma,
            dma((20,)),
        ],
        compiler_params=pltpu.CompilerParams(
            collective_id=0, has_side_effects=True, vmem_limit_bytes=50 * 2**20
        ),
        cost_estimate=pl.CostEstimate(flops=4 * 10**9, bytes_accessed=10 * 2**20, transcendentals=4 * 2**20),
        name="cg_step",
    )(
        coords.T, perm, inv_scale.reshape(1, 64), noise, leaf_basis.T, pair_transfer, coupling,
        solution.T, residual.T, direction.T,
    )
    return tuple(out.T for out in outs)


def solution(mesh):
    rows = P(("group", "within"), None)
    cubes = P(("group", "within"), None, None)
    in_specs = (rows, P(("group", "within")), P(), P(), rows, cubes, cubes, rows, rows, rows)
    return jax.shard_map(
        on_device, mesh=mesh, in_specs=in_specs, out_specs=(rows, rows, rows), check_vma=False
    )
```

```python
import functools
import math

import jax
import jax.numpy as jnp
from jax import lax
from jax.experimental import pallas as pl
from jax.experimental.pallas import tpu as pltpu
from jax.sharding import PartitionSpec as P

LEAF = 512
RANK = 64
COLS = 64
ROWS = 4096
NLEAF = 8
ROOT_FIVE = math.sqrt(5.0)
LN_TWO = math.log(2.0)
MESH = pl.DeviceIdType.MESH
FAR = (4, 3, 5, 2, 6, 1, 7)
F32 = jnp.float32
BF16 = jnp.bfloat16
NT = (((1,), (1,)), ((), ()))
NN = (((1,), (0,)), ((), ()))


def split(a):
    high = a.astype(BF16)
    return high, (a - high.astype(F32)).astype(BF16)


def mxu(a, b, dims=NN):
    return lax.dot_general(a, b, dims, preferred_element_type=F32)


def product(a, b, dims=NN):
    ah, al = split(a)
    bh, bl = split(b)
    return mxu(ah, bh, dims) + (mxu(ah, bl, dims) + mxu(al, bh, dims))


def pack(c):
    half = c.shape[0] // 2
    return jnp.concatenate([c[0:half], c[half:]], axis=1)


def unpack(p):
    return jnp.concatenate([p[:, 0:64], p[:, 64:128]], axis=0)


def raise_pair(transfer, left, right):
    return product(
        jnp.concatenate([left, right], axis=1),
        jnp.concatenate([transfer[:, 0:64], transfer[:, 64:128]], axis=0),
    )


def lower(left, transfer, couple, sibling, state):
    if isinstance(left, bool):
        side = transfer[:, 0:64] if left else transfer[:, 64:128]
        across = couple if left else couple.T
    else:
        side = jnp.where(left, transfer[:, 0:64], transfer[:, 64:128])
        across = jnp.where(left, couple, couple.T)
    none = jnp.zeros((64, 64), F32)
    return product(
        jnp.concatenate([jnp.concatenate([sibling, none], axis=0), state], axis=1),
        jnp.concatenate([across, side], axis=1),
        NT,
    )


def identity():
    row = lax.broadcasted_iota(jnp.int32, (128, 64), 0)
    column = lax.broadcasted_iota(jnp.int32, (128, 64), 1)
    return jnp.where(row == column + 64, 1.0, 0.0)


def lower_tree(mats, coefs):
    near = [identity()]
    for height, first in ((3, 12), (2, 8), (1, 0)):
        below = []
        for k, state in enumerate(near):
            t, b = mats(k * 2**height + 2 ** (height - 1) - 1)
            below.append(lower(True, t, b, coefs(first + 2 * k + 1), state))
            below.append(lower(False, t, b, coefs(first + 2 * k), state))
        near = below
    return jnp.concatenate(near, axis=1)


def kernel(
    coords, order, scale, noise, basis, transfer, coupling, res, direc,
    out_image, out_coef,
    perm, x_in, x_rows, x_perm, b_in, t_in, k_in, r_in, d_in, image,
    d_split, b_split, leaf_c, leaf_f,
    mat_a, mat_z, mat_x, paths, c_a, c_z, c_x, f_top, f_out, pair_c, reduce,
    local_f, local_op, plane_f, plane_op, slab_op,
    in_sem, out_sem, send_sem, rm_a, rm_z, rm_x, r_path, rc_a, rc_z, rc_x, r_f, r_red,
):
    group = lax.axis_index("group")
    within = lax.axis_index("within")
    slab = group
    line = lax.div(within, 8)
    spot = lax.rem(within, 8)
    leader = spot == 7
    top_line = line == 7

    def in_plane(q):
        return (group, line * 8 + q)

    def in_line(q):
        return (group, q * 8 + spot)

    def in_slab(q):
        return (q, within)

    inputs = [
        (transfer, t_in), (coupling, k_in), (direc, d_in), (basis, b_in),
        (coords, x_in), (order, perm), (res, r_in),
    ]
    loads = [
        pltpu.make_async_copy(src, dst, in_sem.at[i]) for i, (src, dst) in enumerate(inputs)
    ]
    for load in loads:
        load.start()

    barrier = pltpu.get_barrier_semaphore()

    def greet(device):
        pl.semaphore_signal(barrier, inc=1, device_id=device, device_id_type=MESH)

    for p in range(1, 8):
        greet(in_plane(lax.rem(spot + p, 8)))
        greet(in_line(lax.rem(line + p, 8)))
    for p in range(1, 4):
        greet(in_slab(lax.rem(slab + p, 4)))

    sends = []

    def remote(src, dst, recv, device):
        index = len(sends)
        copy = pltpu.make_async_remote_copy(
            src_ref=src, dst_ref=dst, send_sem=send_sem.at[index], recv_sem=recv,
            device_id=device, device_id_type=MESH,
        )
        sends.append(copy)
        return copy

    def arrived(dst, recv):
        pltpu.make_async_remote_copy(
            src_ref=dst, dst_ref=dst, send_sem=send_sem.at[0], recv_sem=recv,
            device_id=in_plane(lax.rem(spot + 1, 8)), device_id_type=MESH,
        ).wait_recv()

    loads[0].wait()
    loads[1].wait()
    own = jnp.concatenate([t_in[7], pack(k_in[7])], axis=0)

    @pl.when(jnp.logical_not(leader))
    def _():
        mat_a[spot] = own

    @pl.when(jnp.logical_and(leader, jnp.logical_not(top_line)))
    def _():
        mat_z[line] = own

    @pl.when(jnp.logical_and(leader, top_line))
    def _():
        mat_x[slab] = own

    send_a = [remote(mat_a.at[spot], mat_a.at[spot], rm_a.at[spot], in_plane(7))]
    send_z = [
        remote(mat_z.at[line], mat_z.at[line], rm_z.at[line], in_line(lax.rem(line + p, 8)))
        for p in FAR
    ]
    send_x = [
        remote(mat_x.at[slab], mat_x.at[slab], rm_x.at[slab], in_slab(lax.rem(slab + p, 4)))
        for p in (2, 1, 3)
    ]
    send_p = [remote(paths, paths, r_path, in_line(q)) for q in (3, 4, 2, 5, 1, 6, 0)]

    loads[2].wait()
    loads[3].wait()

    @pl.loop(0, NLEAF)
    def _(leaf):
        at = pl.multiple_of(leaf * LEAF, LEAF)
        dh, dl = split(d_in[:, pl.ds(at, LEAF)])
        bh, bl = split(b_in[:, pl.ds(at, LEAF)])
        both_d = jnp.concatenate([dh, dl], axis=0)
        both_b = jnp.concatenate([bh, bl], axis=0)
        d_split[:, pl.ds(at, LEAF)] = both_d
        b_split[:, pl.ds(at, LEAF)] = both_b
        prod = mxu(both_d, both_b, NT)
        leaf_c[leaf] = (prod[0:64, 0:64] + prod[64:128, 64:128]) + (prod[0:64, 64:128] + prod[64:128, 0:64])

    for k in range(4):
        leaf_c[8 + k] = raise_pair(t_in[2 * k], leaf_c[2 * k], leaf_c[2 * k + 1])
    for k in range(2):
        leaf_c[12 + k] = raise_pair(t_in[4 * k + 1], leaf_c[8 + 2 * k], leaf_c[9 + 2 * k])
    c_a[spot] = pack(raise_pair(t_in[3], leaf_c[12], leaf_c[13]))
    send_ca = [remote(c_a.at[spot], c_a.at[spot], rc_a.at[spot], in_plane(7))]
    owner = jnp.logical_and(jnp.logical_and(leader, top_line), slab < 3)
    pl.semaphore_wait(barrier, 17)
    @pl.when(jnp.logical_not(leader))
    def _():
        for copy in send_ca + send_a:
            copy.start()

    @pl.when(jnp.logical_and(leader, jnp.logical_not(top_line)))
    def _():
        for copy in send_z:
            copy.start()

    @pl.when(owner)
    def _():
        for copy in send_x:
            copy.start()

    local = lower_tree(lambda i: (t_in[i], k_in[i]), lambda i: leaf_c[i])
    local_f[...] = local[0:64]
    local_op[0], local_op[1] = split(local[64:128])

    loads[4].wait()
    loads[5].wait()

    @pl.loop(0, ROWS // 128)
    def _(i):
        at = pl.multiple_of(i * 128, 128)
        x_rows[pl.ds(at, 128), 0:64] = x_in[:, pl.ds(at, 128)].T * (ROOT_FIVE / LN_TWO * scale[...])

    def dense(first, last):
        @pl.loop(first, last)
        def _(leaf):
            at = pl.multiple_of(leaf * LEAF, LEAF)

            @pl.loop(0, LEAF // 32)
            def _(i):
                base = pl.multiple_of(i * 32, 32)
                for j in range(32):
                    x_perm[pl.ds(base + j, 1), :] = x_rows[pl.ds(perm[at + base + j], 1), :]

            xh, xl = split(x_perm[:, 0:64])
            near = xh.astype(F32) + xl.astype(F32)
            square = jnp.sum(near * near, axis=1, keepdims=True)
            square_row = jnp.broadcast_to(square, (LEAF, 128)).T[0:1]
            minus = jnp.asarray(-2.0, BF16)
            one = jnp.concatenate([xh * minus, xh * minus, xl * minus, xl * minus], axis=1)
            two = jnp.concatenate([xh, xl, xh, xl], axis=1)
            vectors = d_split[:, pl.ds(at, LEAF)]
            for c in range(0, LEAF, 256):
                inner = mxu(one, two[c : c + 256], NT)
                dist_sq = jnp.maximum((square + square_row[:, c : c + 256]) + inner, 1e-30)
                dist = dist_sq * lax.rsqrt(dist_sq)
                value = ((1.0 + dist * LN_TWO) + dist_sq * (LN_TWO * LN_TWO / 3.0)) * jnp.exp2(-dist)
                vh, vl = split(value)
                got = mxu(vectors, vh) + mxu(vectors, vl)
                image[:, pl.ds(at + c, 256)] = got[0:64] + got[64:128]

    def mats(ref):
        return ref[0:64, :], unpack(ref[64:96, :])

    def mats(ref):
        return ref[0:64, :], unpack(ref[64:96, :])

    dense(0, 0)

    @pl.when(jnp.logical_and(leader, top_line))
    def _():
        for q in range(3):
            @pl.when(slab != q)
            def _():
                arrived(mat_x.at[q], rm_x.at[q])
        half = lax.div(slab, 2)
        side = lax.rem(slab, 2)
        t, b = mats(mat_x.at[half * 2])
        beside = jnp.where(side == 0, b.T, b)
        turn = jnp.where(side == 0, t[:, 0:64], t[:, 64:128])
        t, b = mats(mat_x.at[1])
        across = product(jnp.where(half == 0, b.T, b), turn, NT)
        t, b = mats(mat_x.at[2 - half * 2])
        paths[...] = pack(
            jnp.concatenate([beside, product(t[:, 0:64], across), product(t[:, 64:128], across)], axis=0)
        )
        for copy in send_p:
            copy.start()

    dense(0, 1)

    send_cz = [
        remote(c_z.at[line], c_z.at[line], rc_z.at[line], in_line(lax.rem(line + p, 8)))
        for p in FAR
    ]
    send_cx = [
        remote(c_x.at[slab], c_x.at[slab], rc_x.at[slab], in_slab(lax.rem(slab + p, 4)))
        for p in (2, 1, 3)
    ]
    send_f = [remote(f_out.at[q], f_top, r_f, in_plane(q)) for q in range(7)]

    @pl.when(leader)
    def _():
        for q in range(7):
            arrived(c_a.at[q], rc_a.at[q])
            arrived(mat_a.at[q], rm_a.at[q])
        for k in range(8):
            pair_c[k] = unpack(c_a[k])
        for k in range(4):
            pair_c[8 + k] = raise_pair(mat_a[2 * k, 0:64, :], pair_c[2 * k], pair_c[2 * k + 1])
        for k in range(2):
            pair_c[12 + k] = raise_pair(mat_a[4 * k + 1, 0:64, :], pair_c[8 + 2 * k], pair_c[9 + 2 * k])
        c_z[line] = pack(raise_pair(mat_a[3, 0:64, :], pair_c[12], pair_c[13]))
        for copy in send_cz:
            copy.start()
        plane = lower_tree(lambda i: mats(mat_a.at[i]), lambda i: pair_c[i])
        plane_f[...] = plane[0:64]
        plane_op[...] = plane[64:128]

    dense(1, 3)

    @pl.when(leader)
    def _():
        for p in range(1, 8):
            q = lax.rem(line + p, 8)
            arrived(c_z.at[q], rc_z.at[q])

            @pl.when(q != 7)
            def _():
                arrived(mat_z.at[q], rm_z.at[q])
        for k in range(8):
            pair_c[k] = unpack(c_z[k])
        for k in range(4):
            pair_c[8 + k] = raise_pair(mat_z[2 * k, 0:64, :], pair_c[2 * k], pair_c[2 * k + 1])
        for k in range(2):
            pair_c[12 + k] = raise_pair(mat_z[4 * k + 1, 0:64, :], pair_c[8 + 2 * k], pair_c[9 + 2 * k])
        c_x[slab] = pack(raise_pair(mat_z[3, 0:64, :], pair_c[12], pair_c[13]))
        for copy in send_cx:
            copy.start()

        half = lax.div(line, 4)
        quarter = lax.div(line, 2)
        t, b = mats(mat_z.at[3])
        state = lower(half == 0, t, b, pair_c[13 - half], identity())
        side = lax.rem(quarter, 2)
        t, b = mats(mat_z.at[half * 4 + 1])
        state = lower(side == 0, t, b, pair_c[8 + half * 2 + 1 - side], state)
        side = lax.rem(line, 2)
        t, b = mats(mat_z.at[quarter * 2])
        state = lower(side == 0, t, b, pair_c[quarter * 2 + 1 - side], state)
        both = product(state, plane_op[...])
        plane_f[...] = plane_f[...] + both[0:64]

        @pl.when(jnp.logical_not(top_line))
        def _():
            arrived(paths, r_path)
        slab_op[0], slab_op[1] = split(product(unpack(paths[...]), both[64:128]))

    dense(3, 5)

    @pl.when(leader)
    def _():
        for p in range(1, 4):
            q = lax.rem(slab + p, 4)
            arrived(c_x.at[q], rc_x.at[q])
        half = lax.div(slab, 2)
        others = (half * 2 + 1 - lax.rem(slab, 2), 2 - half * 2, 3 - half * 2)
        ch, cl = split(jnp.concatenate([unpack(c_x[q]) for q in others], axis=1))
        far = plane_f[...] + (mxu(ch, slab_op[0]) + (mxu(ch, slab_op[1]) + mxu(cl, slab_op[0])))
        for q in range(8):
            f_out[q] = pack(far[:, q * 64 : q * 64 + 64])
        for copy in send_f:
            copy.start()
        f_top[...] = f_out[7]

    dense(5, 8)

    @pl.when(jnp.logical_not(leader))
    def _():
        arrived(f_top, r_f)
    fh, fl = split(unpack(f_top[...]))
    far = local_f[...] + (mxu(fh, local_op[0]) + (mxu(fh, local_op[1]) + mxu(fl, local_op[0])))
    for k in range(NLEAF):
        fh, fl = split(far[:, k * 64 : k * 64 + 64])
        leaf_f[k] = jnp.concatenate(
            [jnp.concatenate([fh, fh], axis=1), jnp.concatenate([fl, fl], axis=1)], axis=0
        )

    loads[6].wait()
    shift = noise[0]
    zero = jnp.zeros((COLS, 128), F32)

    def store(leaf):
        at = pl.multiple_of(leaf * LEAF, LEAF)
        return pltpu.make_async_copy(
            image.at[:, pl.ds(at, LEAF)], out_image.at[:, pl.ds(at, LEAF)], out_sem.at[leaf]
        )

    def add_leaf(leaf, sums):
        at = pl.multiple_of(leaf * LEAF, LEAF)
        far = mxu(leaf_f[leaf], b_split[:, pl.ds(at, LEAF)])
        d = d_in[:, pl.ds(at, LEAF)]
        r = r_in[:, pl.ds(at, LEAF)]
        q = image[:, pl.ds(at, LEAF)] + shift * d + (far[0:64] + far[64:128])
        image[:, pl.ds(at, LEAF)] = q
        store(leaf).start()
        terms = (r * r, d * q, r * q, q * q)
        return tuple(
            total + ((term[:, 0:128] + term[:, 128:256]) + (term[:, 256:384] + term[:, 384:512]))
            for total, term in zip(sums, terms)
        )

    sums = lax.fori_loop(0, NLEAF, add_leaf, (zero, zero, zero, zero))
    lane = lax.broadcasted_iota(jnp.int32, (COLS, 128), 1)
    table = zero
    for i, total in enumerate(sums):
        table = jnp.where(lane == i, jnp.sum(total, axis=1, keepdims=True), table)
    value = table.T[0:8, :]

    first = 0
    send_red = []
    for size, place, device in ((8, spot, in_plane), (8, line, in_line), (4, slab, in_slab)):
        reduce[first + place, :, 0:64] = value
        copies = []
        for p in FAR if size == 8 else (2, 1, 3):
            q = lax.rem(place + p, size)
            copies.append(
                remote(reduce.at[first + place], reduce.at[first + place], r_red.at[first + place], device(q))
            )
        for copy in copies:
            copy.start()
        send_red.extend(copies)
        for p in range(1, size):
            q = lax.rem(place + p, size)
            arrived(reduce.at[first + q], r_red.at[first + q])
        value = reduce[first, :, 0:64]
        for q in range(1, size):
            value = value + reduce[first + q, :, 0:64]
        first += size

    old, curve, cross, own_square = value[0:1], value[1:2], value[2:3], value[3:4]
    alpha = old / curve
    new = old - 2.0 * alpha * cross + alpha * alpha * own_square
    ratio = new / old
    out_coef[0] = jnp.broadcast_to(alpha, (128, COLS)).T
    out_coef[1] = jnp.broadcast_to(ratio, (128, COLS)).T

    for copy in send_red:
        copy.wait_send()

    @pl.when(jnp.logical_not(leader))
    def _():
        for copy in send_ca + send_a:
            copy.wait_send()

    @pl.when(leader)
    def _():
        for copy in send_cz + send_cx + send_f:
            copy.wait_send()

    @pl.when(jnp.logical_and(leader, jnp.logical_not(top_line)))
    def _():
        for copy in send_z:
            copy.wait_send()

    @pl.when(owner)
    def _():
        for copy in send_x:
            copy.wait_send()

    @pl.when(jnp.logical_and(leader, top_line))
    def _():
        for copy in send_p:
            copy.wait_send()

    @pl.loop(0, NLEAF)
    def _(leaf):
        store(leaf).wait()


def finish(coef, image, sol, res, direc, out_sol, out_res, out_dir, held, made, in_sem, out_sem):
    parts = in_sem.shape[1]
    width = ROWS // parts
    alpha = jnp.concatenate([coef[0]] * (width // 128), axis=1)
    ratio = jnp.concatenate([coef[1]] * (width // 128), axis=1)
    loads = [
        [
            pltpu.make_async_copy(
                src.at[:, pl.ds(k * width, width)], held.at[i, :, pl.ds(k * width, width)], in_sem.at[i, k]
            )
            for i, src in enumerate((image, sol, res, direc))
        ]
        for k in range(parts)
    ]
    stores = [
        [
            pltpu.make_async_copy(
                made.at[i, :, pl.ds(k * width, width)], dst.at[:, pl.ds(k * width, width)], out_sem.at[i, k]
            )
            for i, dst in enumerate((out_sol, out_res, out_dir))
        ]
        for k in range(parts)
    ]
    for part in loads:
        for load in part:
            load.start()
    for k in range(parts):
        for load in loads[k]:
            load.wait()
        at = pl.ds(k * width, width)
        d = held[3, :, at]
        r = held[2, :, at] - alpha * held[0, :, at]
        made[0, :, at] = held[1, :, at] + alpha * d
        made[1, :, at] = r
        made[2, :, at] = r + ratio * d
        for store in stores[k]:
            store.start()
    for part in stores:
        for store in part:
            store.wait()


def on_device(
    coords, perm, inv_scale, noise, leaf_basis, pair_transfer, coupling, solution, residual, direction
):
    hbm = pl.BlockSpec(memory_space=pltpu.HBM)
    anywhere = pl.BlockSpec(memory_space=pl.ANY)
    smem = pl.BlockSpec(memory_space=pltpu.SMEM)
    vmem = pl.BlockSpec(memory_space=pltpu.VMEM)
    wide = jax.ShapeDtypeStruct((COLS, ROWS), F32)
    dma = pltpu.SemaphoreType.DMA
    image, coef = pl.pallas_call(
        kernel,
        out_shape=(wide, jax.ShapeDtypeStruct((2, COLS, 128), F32)),
        in_specs=[hbm, hbm, vmem, smem, hbm, hbm, hbm, hbm, hbm],
        out_specs=(anywhere, vmem),
        scratch_shapes=[
            pltpu.SMEM((ROWS,), jnp.int32),
            pltpu.VMEM((64, ROWS), F32),
            pltpu.VMEM((ROWS, 128), F32),
            pltpu.VMEM((LEAF, 128), F32),
            pltpu.VMEM((64, ROWS), F32),
            pltpu.VMEM((8, 64, 128), F32),
            pltpu.VMEM((8, 64, 64), F32),
            pltpu.VMEM((64, ROWS), F32),
            pltpu.VMEM((64, ROWS), F32),
            pltpu.VMEM((64, ROWS), F32),
            pltpu.VMEM((128, ROWS), BF16),
            pltpu.VMEM((128, ROWS), BF16),
            pltpu.VMEM((14, 64, 64), F32),
            pltpu.VMEM((8, 128, 128), BF16),
            pltpu.VMEM((8, 96, 128), F32),
            pltpu.VMEM((8, 96, 128), F32),
            pltpu.VMEM((4, 96, 128), F32),
            pltpu.VMEM((96, 128), F32),
            pltpu.VMEM((8, 32, 128), F32),
            pltpu.VMEM((8, 32, 128), F32),
            pltpu.VMEM((4, 32, 128), F32),
            pltpu.VMEM((32, 128), F32),
            pltpu.VMEM((8, 32, 128), F32),
            pltpu.VMEM((14, 64, 64), F32),
            pltpu.VMEM((20, 8, 128), F32),
            pltpu.VMEM((64, LEAF), F32),
            pltpu.VMEM((2, 64, LEAF), BF16),
            pltpu.VMEM((64, LEAF), F32),
            pltpu.VMEM((64, LEAF), F32),
            pltpu.VMEM((2, 192, LEAF), BF16),
            dma((7,)),
            dma((NLEAF,)),
            dma((96,)),
            dma((8,)),
            dma((8,)),
            dma((4,)),
            dma,
            dma((8,)),
            dma((8,)),
            dma((4,)),
            dma,
            dma((20,)),
        ],
        compiler_params=pltpu.CompilerParams(
            collective_id=0, has_side_effects=True, vmem_limit_bytes=60 * 2**20
        ),
        cost_estimate=pl.CostEstimate(flops=4 * 10**9, bytes_accessed=10 * 2**20, transcendentals=4 * 2**20),
        name="cg_step",
    )(
        coords.T, perm, inv_scale.reshape(1, 64), noise, leaf_basis.T, pair_transfer, coupling,
        residual.T, direction.T,
    )
    parts = 4
    outs = pl.pallas_call(
        finish,
        out_shape=(wide, wide, wide),
        in_specs=[vmem, anywhere, anywhere, anywhere, anywhere],
        out_specs=(anywhere, anywhere, anywhere),
        scratch_shapes=[
            pltpu.VMEM((4, COLS, ROWS), F32),
            pltpu.VMEM((3, COLS, ROWS), F32),
            dma((4, parts)),
            dma((3, parts)),
        ],
        compiler_params=pltpu.CompilerParams(vmem_limit_bytes=60 * 2**20),
        name="cg_finish",
    )(coef, image, solution.T, residual.T, direction.T)
    return tuple(out.T for out in outs)


def solution(mesh):
    rows = P(("group", "within"), None)
    cubes = P(("group", "within"), None, None)
    in_specs = (rows, P(("group", "within")), P(), P(), rows, cubes, cubes, rows, rows, rows)
    return jax.shard_map(
        on_device, mesh=mesh, in_specs=in_specs, out_specs=(rows, rows, rows), check_vma=False
    )
```

```python
import functools
import math

import jax
import jax.numpy as jnp
from jax import lax
from jax.experimental import pallas as pl
from jax.experimental.pallas import tpu as pltpu
from jax.sharding import PartitionSpec as P

LEAF = 512
RANK = 64
COLS = 64
ROWS = 4096
NLEAF = 8
ROOT_FIVE = math.sqrt(5.0)
LN_TWO = math.log(2.0)
MESH = pl.DeviceIdType.MESH
FAR = (4, 3, 5, 2, 6, 1, 7)
F32 = jnp.float32
BF16 = jnp.bfloat16
NT = (((1,), (1,)), ((), ()))
NN = (((1,), (0,)), ((), ()))


def split(a):
    high = a.astype(BF16)
    return high, (a - high.astype(F32)).astype(BF16)


def mxu(a, b, dims=NN):
    return lax.dot_general(a, b, dims, preferred_element_type=F32)


def product(a, b, dims=NN):
    ah, al = split(a)
    bh, bl = split(b)
    axis = 1 if dims == NT else 0
    both = mxu(jnp.concatenate([ah, al], axis=1), jnp.concatenate([bh, bh], axis=axis), dims)
    return both + mxu(ah, bl, dims)


def pack(c):
    half = c.shape[0] // 2
    return jnp.concatenate([c[0:half], c[half:]], axis=1)


def unpack(p):
    return jnp.concatenate([p[:, 0:64], p[:, 64:128]], axis=0)


def raise_pair(transfer, left, right):
    return product(
        jnp.concatenate([left, right], axis=1),
        jnp.concatenate([transfer[:, 0:64], transfer[:, 64:128]], axis=0),
    )


def lower(left, transfer, couple, sibling, state):
    if isinstance(left, bool):
        side = transfer[:, 0:64] if left else transfer[:, 64:128]
        across = couple if left else couple.T
    else:
        side = jnp.where(left, transfer[:, 0:64], transfer[:, 64:128])
        across = jnp.where(left, couple, couple.T)
    none = jnp.zeros((64, 64), F32)
    return product(
        jnp.concatenate([jnp.concatenate([sibling, none], axis=0), state], axis=1),
        jnp.concatenate([across, side], axis=1),
        NT,
    )


def identity():
    row = lax.broadcasted_iota(jnp.int32, (128, 64), 0)
    column = lax.broadcasted_iota(jnp.int32, (128, 64), 1)
    return jnp.where(row == column + 64, 1.0, 0.0)


def lower_tree(mats, coefs):
    near = [identity()]
    for height, first in ((3, 12), (2, 8), (1, 0)):
        below = []
        for k, state in enumerate(near):
            t, b = mats(k * 2**height + 2 ** (height - 1) - 1)
            below.append(lower(True, t, b, coefs(first + 2 * k + 1), state))
            below.append(lower(False, t, b, coefs(first + 2 * k), state))
        near = below
    return jnp.concatenate(near, axis=1)


def kernel(
    coords, order, scale, noise, basis, transfer, coupling, res, direc,
    out_image, out_coef,
    perm, x_in, x_rows, x_perm, b_in, t_in, k_in, r_in, d_in, image,
    d_split, b_split, leaf_c, leaf_f,
    mat_a, mat_z, mat_x, paths, c_a, c_z, c_x, f_top, f_out, pair_c, reduce,
    local_f, local_op, plane_f, plane_op, slab_op,
    in_sem, out_sem, send_sem, rm_a, rm_z, rm_x, r_path, rc_a, rc_z, rc_x, r_f, r_red,
):
    group = lax.axis_index("group")
    within = lax.axis_index("within")
    slab = group
    line = lax.div(within, 8)
    spot = lax.rem(within, 8)
    leader = spot == 7
    top_line = line == 7

    def in_plane(q):
        return (group, line * 8 + q)

    def in_line(q):
        return (group, q * 8 + spot)

    def in_slab(q):
        return (q, within)

    inputs = [
        (transfer, t_in), (coupling, k_in), (direc, d_in), (basis, b_in),
        (coords, x_in), (order, perm), (res, r_in),
    ]
    loads = [
        pltpu.make_async_copy(src, dst, in_sem.at[i]) for i, (src, dst) in enumerate(inputs)
    ]
    for load in loads:
        load.start()

    barrier = pltpu.get_barrier_semaphore()

    def greet(device):
        pl.semaphore_signal(barrier, inc=1, device_id=device, device_id_type=MESH)

    for p in range(1, 8):
        greet(in_plane(lax.rem(spot + p, 8)))
        greet(in_line(lax.rem(line + p, 8)))
    for p in range(1, 4):
        greet(in_slab(lax.rem(slab + p, 4)))

    sends = []

    def remote(src, dst, recv, device):
        index = len(sends)
        copy = pltpu.make_async_remote_copy(
            src_ref=src, dst_ref=dst, send_sem=send_sem.at[index], recv_sem=recv,
            device_id=device, device_id_type=MESH,
        )
        sends.append(copy)
        return copy

    def arrived(dst, recv):
        pltpu.make_async_remote_copy(
            src_ref=dst, dst_ref=dst, send_sem=send_sem.at[0], recv_sem=recv,
            device_id=in_plane(lax.rem(spot + 1, 8)), device_id_type=MESH,
        ).wait_recv()

    loads[0].wait()
    loads[1].wait()
    own = jnp.concatenate([t_in[7], pack(k_in[7])], axis=0)

    @pl.when(jnp.logical_not(leader))
    def _():
        mat_a[spot] = own

    @pl.when(jnp.logical_and(leader, jnp.logical_not(top_line)))
    def _():
        mat_z[line] = own

    @pl.when(jnp.logical_and(leader, top_line))
    def _():
        mat_x[slab] = own

    send_a = [remote(mat_a.at[spot], mat_a.at[spot], rm_a.at[spot], in_plane(7))]
    send_z = [
        remote(mat_z.at[line], mat_z.at[line], rm_z.at[line], in_line(lax.rem(line + p, 8)))
        for p in FAR
    ]
    send_x = [
        remote(mat_x.at[slab], mat_x.at[slab], rm_x.at[slab], in_slab(lax.rem(slab + p, 4)))
        for p in (2, 1, 3)
    ]
    send_p = [remote(paths, paths, r_path, in_line(q)) for q in (3, 4, 2, 5, 1, 6, 0)]

    loads[2].wait()
    loads[3].wait()

    @pl.loop(0, NLEAF)
    def _(leaf):
        at = pl.multiple_of(leaf * LEAF, LEAF)
        dh, dl = split(d_in[:, pl.ds(at, LEAF)])
        bh, bl = split(b_in[:, pl.ds(at, LEAF)])
        both_d = jnp.concatenate([dh, dl], axis=0)
        both_b = jnp.concatenate([bh, bl], axis=0)
        d_split[:, pl.ds(at, LEAF)] = both_d
        b_split[:, pl.ds(at, LEAF)] = both_b
        prod = mxu(both_d, both_b, NT)
        leaf_c[leaf] = (prod[0:64, 0:64] + prod[64:128, 64:128]) + (prod[0:64, 64:128] + prod[64:128, 0:64])

    for k in range(4):
        leaf_c[8 + k] = raise_pair(t_in[2 * k], leaf_c[2 * k], leaf_c[2 * k + 1])
    for k in range(2):
        leaf_c[12 + k] = raise_pair(t_in[4 * k + 1], leaf_c[8 + 2 * k], leaf_c[9 + 2 * k])
    c_a[spot] = pack(raise_pair(t_in[3], leaf_c[12], leaf_c[13]))
    send_ca = [remote(c_a.at[spot], c_a.at[spot], rc_a.at[spot], in_plane(7))]
    owner = jnp.logical_and(jnp.logical_and(leader, top_line), slab < 3)
    pl.semaphore_wait(barrier, 17)
    @pl.when(jnp.logical_not(leader))
    def _():
        for copy in send_ca + send_a:
            copy.start()

    @pl.when(jnp.logical_and(leader, jnp.logical_not(top_line)))
    def _():
        for copy in send_z:
            copy.start()

    @pl.when(owner)
    def _():
        for copy in send_x:
            copy.start()

    loads[4].wait()
    loads[5].wait()

    @pl.loop(0, ROWS // 128)
    def _(i):
        at = pl.multiple_of(i * 128, 128)
        x_rows[pl.ds(at, 128), 0:64] = x_in[:, pl.ds(at, 128)].T * (ROOT_FIVE / LN_TWO * scale[...])

    def gather(at, first, count):
        for j in range(first, first + count):
            x_perm[pl.ds(j, 1), :] = x_rows[pl.ds(perm[at + j], 1), :]

    @pl.loop(0, LEAF // 64)
    def _(i):
        base = pl.multiple_of(i * 64, 64)
        for j in range(64):
            x_perm[pl.ds(base + j, 1), :] = x_rows[pl.ds(perm[base + j], 1), :]

    def dense(first, last):
        @pl.loop(first, last)
        def _(leaf):
            at = pl.multiple_of(leaf * LEAF, LEAF)

            xh, xl = split(x_perm[:, 0:64])
            near = xh.astype(F32) + xl.astype(F32)
            square = jnp.sum(near * near, axis=1, keepdims=True)
            square_row = jnp.broadcast_to(square, (LEAF, 128)).T[0:1]
            minus = jnp.asarray(-2.0, BF16)
            one = jnp.concatenate([xh * minus, xh * minus, xl * minus, xl * minus], axis=1)
            two = jnp.concatenate([xh, xl, xh, xl], axis=1)
            vectors = d_split[:, pl.ds(at, LEAF)]
            following = jnp.minimum(at + LEAF, ROWS - LEAF)
            for c in range(0, LEAF, 256):
                gather(following, c, 256)
                inner = mxu(one, two[c : c + 256], NT)
                dist_sq = jnp.maximum((square + square_row[:, c : c + 256]) + inner, 1e-30)
                dist = dist_sq * lax.rsqrt(dist_sq)
                value = ((1.0 + dist * LN_TWO) + dist_sq * (LN_TWO * LN_TWO / 3.0)) * jnp.exp2(-dist)
                vh, vl = split(value)
                got = mxu(vectors, vh)
                image[:, pl.ds(at + c, 256)] = got[0:64] + (got[64:128] + mxu(vectors[0:64], vl))

    def mats(ref):
        return ref[0:64, :], unpack(ref[64:96, :])

    def mats(ref):
        return ref[0:64, :], unpack(ref[64:96, :])

    dense(0, 0)

    @pl.when(jnp.logical_and(leader, top_line))
    def _():
        for q in range(3):
            @pl.when(slab != q)
            def _():
                arrived(mat_x.at[q], rm_x.at[q])
        half = lax.div(slab, 2)
        side = lax.rem(slab, 2)
        t, b = mats(mat_x.at[half * 2])
        beside = jnp.where(side == 0, b.T, b)
        turn = jnp.where(side == 0, t[:, 0:64], t[:, 64:128])
        t, b = mats(mat_x.at[1])
        across = product(jnp.where(half == 0, b.T, b), turn, NT)
        t, b = mats(mat_x.at[2 - half * 2])
        paths[...] = pack(
            jnp.concatenate([beside, product(t[:, 0:64], across), product(t[:, 64:128], across)], axis=0)
        )
        for copy in send_p:
            copy.start()

    dense(0, 1)

    send_cz = [
        remote(c_z.at[line], c_z.at[line], rc_z.at[line], in_line(lax.rem(line + p, 8)))
        for p in FAR
    ]
    send_cx = [
        remote(c_x.at[slab], c_x.at[slab], rc_x.at[slab], in_slab(lax.rem(slab + p, 4)))
        for p in (2, 1, 3)
    ]
    send_f = [remote(f_out.at[q], f_top, r_f, in_plane(q)) for q in range(7)]

    @pl.when(leader)
    def _():
        for q in range(7):
            arrived(c_a.at[q], rc_a.at[q])
            arrived(mat_a.at[q], rm_a.at[q])
        for k in range(8):
            pair_c[k] = unpack(c_a[k])
        for k in range(4):
            pair_c[8 + k] = raise_pair(mat_a[2 * k, 0:64, :], pair_c[2 * k], pair_c[2 * k + 1])
        for k in range(2):
            pair_c[12 + k] = raise_pair(mat_a[4 * k + 1, 0:64, :], pair_c[8 + 2 * k], pair_c[9 + 2 * k])
        c_z[line] = pack(raise_pair(mat_a[3, 0:64, :], pair_c[12], pair_c[13]))
        for copy in send_cz:
            copy.start()
        plane = lower_tree(lambda i: mats(mat_a.at[i]), lambda i: pair_c[i])
        plane_f[...] = plane[0:64]
        plane_op[...] = plane[64:128]

    dense(1, 4)

    @pl.when(leader)
    def _():
        for p in range(1, 8):
            q = lax.rem(line + p, 8)
            arrived(c_z.at[q], rc_z.at[q])

            @pl.when(q != 7)
            def _():
                arrived(mat_z.at[q], rm_z.at[q])
        for k in range(8):
            pair_c[k] = unpack(c_z[k])
        for k in range(4):
            pair_c[8 + k] = raise_pair(mat_z[2 * k, 0:64, :], pair_c[2 * k], pair_c[2 * k + 1])
        for k in range(2):
            pair_c[12 + k] = raise_pair(mat_z[4 * k + 1, 0:64, :], pair_c[8 + 2 * k], pair_c[9 + 2 * k])
        c_x[slab] = pack(raise_pair(mat_z[3, 0:64, :], pair_c[12], pair_c[13]))
        for copy in send_cx:
            copy.start()

        half = lax.div(line, 4)
        quarter = lax.div(line, 2)
        t, b = mats(mat_z.at[3])
        state = lower(half == 0, t, b, pair_c[13 - half], identity())
        side = lax.rem(quarter, 2)
        t, b = mats(mat_z.at[half * 4 + 1])
        state = lower(side == 0, t, b, pair_c[8 + half * 2 + 1 - side], state)
        side = lax.rem(line, 2)
        t, b = mats(mat_z.at[quarter * 2])
        state = lower(side == 0, t, b, pair_c[quarter * 2 + 1 - side], state)
        both = product(state, plane_op[...])
        plane_f[...] = plane_f[...] + both[0:64]

        @pl.when(jnp.logical_not(top_line))
        def _():
            arrived(paths, r_path)
        slab_op[0], slab_op[1] = split(product(unpack(paths[...]), both[64:128]))

    dense(4, 6)

    @pl.when(leader)
    def _():
        for p in range(1, 4):
            q = lax.rem(slab + p, 4)
            arrived(c_x.at[q], rc_x.at[q])
        half = lax.div(slab, 2)
        others = (half * 2 + 1 - lax.rem(slab, 2), 2 - half * 2, 3 - half * 2)
        ch, cl = split(jnp.concatenate([unpack(c_x[q]) for q in others], axis=1))
        far = plane_f[...] + (mxu(ch, slab_op[0]) + (mxu(ch, slab_op[1]) + mxu(cl, slab_op[0])))
        for q in range(8):
            f_out[q] = pack(far[:, q * 64 : q * 64 + 64])
        for copy in send_f:
            copy.start()
        f_top[...] = f_out[7]

    local = lower_tree(lambda i: (t_in[i], k_in[i]), lambda i: leaf_c[i])
    local_f[...] = local[0:64]
    local_op[0], local_op[1] = split(local[64:128])

    dense(6, 8)

    @pl.when(jnp.logical_not(leader))
    def _():
        arrived(f_top, r_f)
    fh, fl = split(unpack(f_top[...]))
    far = local_f[...] + (mxu(fh, local_op[0]) + (mxu(fh, local_op[1]) + mxu(fl, local_op[0])))
    for k in range(NLEAF):
        fh, fl = split(far[:, k * 64 : k * 64 + 64])
        leaf_f[k] = jnp.concatenate(
            [jnp.concatenate([fh, fh], axis=1), jnp.concatenate([fl, fl], axis=1)], axis=0
        )

    loads[6].wait()
    shift = noise[0]
    zero = jnp.zeros((COLS, 128), F32)

    def store(leaf):
        at = pl.multiple_of(leaf * LEAF, LEAF)
        return pltpu.make_async_copy(
            image.at[:, pl.ds(at, LEAF)], out_image.at[:, pl.ds(at, LEAF)], out_sem.at[leaf]
        )

    def add_leaf(leaf, sums):
        at = pl.multiple_of(leaf * LEAF, LEAF)
        far = mxu(leaf_f[leaf], b_split[:, pl.ds(at, LEAF)])
        d = d_in[:, pl.ds(at, LEAF)]
        r = r_in[:, pl.ds(at, LEAF)]
        q = image[:, pl.ds(at, LEAF)] + shift * d + (far[0:64] + far[64:128])
        image[:, pl.ds(at, LEAF)] = q
        store(leaf).start()
        terms = (r * r, d * q, r * q, q * q)
        return tuple(
            total + ((term[:, 0:128] + term[:, 128:256]) + (term[:, 256:384] + term[:, 384:512]))
            for total, term in zip(sums, terms)
        )

    sums = lax.fori_loop(0, NLEAF, add_leaf, (zero, zero, zero, zero))
    lane = lax.broadcasted_iota(jnp.int32, (COLS, 128), 1)
    table = zero
    for i, total in enumerate(sums):
        table = jnp.where(lane == i, jnp.sum(total, axis=1, keepdims=True), table)
    value = table.T[0:8, :]

    first = 0
    send_red = []
    for size, place, device in ((8, spot, in_plane), (8, line, in_line), (4, slab, in_slab)):
        reduce[first + place, :, 0:64] = value
        copies = []
        for p in FAR if size == 8 else (2, 1, 3):
            q = lax.rem(place + p, size)
            copies.append(
                remote(reduce.at[first + place], reduce.at[first + place], r_red.at[first + place], device(q))
            )
        for copy in copies:
            copy.start()
        send_red.extend(copies)
        for p in range(1, size):
            q = lax.rem(place + p, size)
            arrived(reduce.at[first + q], r_red.at[first + q])
        value = reduce[first, :, 0:64]
        for q in range(1, size):
            value = value + reduce[first + q, :, 0:64]
        first += size

    old, curve, cross, own_square = value[0:1], value[1:2], value[2:3], value[3:4]
    alpha = old / curve
    new = old - 2.0 * alpha * cross + alpha * alpha * own_square
    ratio = new / old
    out_coef[0] = jnp.broadcast_to(alpha, (128, COLS)).T
    out_coef[1] = jnp.broadcast_to(ratio, (128, COLS)).T

    for copy in send_red:
        copy.wait_send()

    @pl.when(jnp.logical_not(leader))
    def _():
        for copy in send_ca + send_a:
            copy.wait_send()

    @pl.when(leader)
    def _():
        for copy in send_cz + send_cx + send_f:
            copy.wait_send()

    @pl.when(jnp.logical_and(leader, jnp.logical_not(top_line)))
    def _():
        for copy in send_z:
            copy.wait_send()

    @pl.when(owner)
    def _():
        for copy in send_x:
            copy.wait_send()

    @pl.when(jnp.logical_and(leader, top_line))
    def _():
        for copy in send_p:
            copy.wait_send()

    @pl.loop(0, NLEAF)
    def _(leaf):
        store(leaf).wait()


def finish(coef, image, sol, res, direc, out_sol, out_res, out_dir, held, made, in_sem, out_sem):
    parts = in_sem.shape[1]
    width = ROWS // parts
    alpha = jnp.concatenate([coef[0]] * (width // 128), axis=1)
    ratio = jnp.concatenate([coef[1]] * (width // 128), axis=1)
    loads = [
        [
            pltpu.make_async_copy(
                src.at[:, pl.ds(k * width, width)], held.at[i, :, pl.ds(k * width, width)], in_sem.at[i, k]
            )
            for i, src in enumerate((image, sol, res, direc))
        ]
        for k in range(parts)
    ]
    stores = [
        [
            pltpu.make_async_copy(
                made.at[i, :, pl.ds(k * width, width)], dst.at[:, pl.ds(k * width, width)], out_sem.at[i, k]
            )
            for i, dst in enumerate((out_sol, out_res, out_dir))
        ]
        for k in range(parts)
    ]
    for part in loads:
        for load in part:
            load.start()
    for k in range(parts):
        for load in loads[k]:
            load.wait()
        at = pl.ds(k * width, width)
        d = held[3, :, at]
        r = held[2, :, at] - alpha * held[0, :, at]
        made[0, :, at] = held[1, :, at] + alpha * d
        made[1, :, at] = r
        made[2, :, at] = r + ratio * d
        for store in stores[k]:
            store.start()
    for part in stores:
        for store in part:
            store.wait()


def on_device(
    coords, perm, inv_scale, noise, leaf_basis, pair_transfer, coupling, solution, residual, direction
):
    hbm = pl.BlockSpec(memory_space=pltpu.HBM)
    anywhere = pl.BlockSpec(memory_space=pl.ANY)
    smem = pl.BlockSpec(memory_space=pltpu.SMEM)
    vmem = pl.BlockSpec(memory_space=pltpu.VMEM)
    wide = jax.ShapeDtypeStruct((COLS, ROWS), F32)
    dma = pltpu.SemaphoreType.DMA
    image, coef = pl.pallas_call(
        kernel,
        out_shape=(wide, jax.ShapeDtypeStruct((2, COLS, 128), F32)),
        in_specs=[hbm, hbm, vmem, smem, hbm, hbm, hbm, hbm, hbm],
        out_specs=(anywhere, vmem),
        scratch_shapes=[
            pltpu.SMEM((ROWS,), jnp.int32),
            pltpu.VMEM((64, ROWS), F32),
            pltpu.VMEM((ROWS, 128), F32),
            pltpu.VMEM((LEAF, 128), F32),
            pltpu.VMEM((64, ROWS), F32),
            pltpu.VMEM((8, 64, 128), F32),
            pltpu.VMEM((8, 64, 64), F32),
            pltpu.VMEM((64, ROWS), F32),
            pltpu.VMEM((64, ROWS), F32),
            pltpu.VMEM((64, ROWS), F32),
            pltpu.VMEM((128, ROWS), BF16),
            pltpu.VMEM((128, ROWS), BF16),
            pltpu.VMEM((14, 64, 64), F32),
            pltpu.VMEM((8, 128, 128), BF16),
            pltpu.VMEM((8, 96, 128), F32),
            pltpu.VMEM((8, 96, 128), F32),
            pltpu.VMEM((4, 96, 128), F32),
            pltpu.VMEM((96, 128), F32),
            pltpu.VMEM((8, 32, 128), F32),
            pltpu.VMEM((8, 32, 128), F32),
            pltpu.VMEM((4, 32, 128), F32),
            pltpu.VMEM((32, 128), F32),
            pltpu.VMEM((8, 32, 128), F32),
            pltpu.VMEM((14, 64, 64), F32),
            pltpu.VMEM((20, 8, 128), F32),
            pltpu.VMEM((64, LEAF), F32),
            pltpu.VMEM((2, 64, LEAF), BF16),
            pltpu.VMEM((64, LEAF), F32),
            pltpu.VMEM((64, LEAF), F32),
            pltpu.VMEM((2, 192, LEAF), BF16),
            dma((7,)),
            dma((NLEAF,)),
            dma((96,)),
            dma((8,)),
            dma((8,)),
            dma((4,)),
            dma,
            dma((8,)),
            dma((8,)),
            dma((4,)),
            dma,
            dma((20,)),
        ],
        compiler_params=pltpu.CompilerParams(
            collective_id=0, has_side_effects=True, vmem_limit_bytes=60 * 2**20
        ),
        cost_estimate=pl.CostEstimate(flops=4 * 10**9, bytes_accessed=10 * 2**20, transcendentals=4 * 2**20),
        name="cg_step",
    )(
        coords.T, perm, inv_scale.reshape(1, 64), noise, leaf_basis.T, pair_transfer, coupling,
        residual.T, direction.T,
    )
    parts = 4
    outs = pl.pallas_call(
        finish,
        out_shape=(wide, wide, wide),
        in_specs=[vmem, anywhere, anywhere, anywhere, anywhere],
        out_specs=(anywhere, anywhere, anywhere),
        scratch_shapes=[
            pltpu.VMEM((4, COLS, ROWS), F32),
            pltpu.VMEM((3, COLS, ROWS), F32),
            dma((4, parts)),
            dma((3, parts)),
        ],
        compiler_params=pltpu.CompilerParams(vmem_limit_bytes=60 * 2**20),
        name="cg_finish",
    )(coef, image, solution.T, residual.T, direction.T)
    return tuple(out.T for out in outs)


def solution(mesh):
    rows = P(("group", "within"), None)
    cubes = P(("group", "within"), None, None)
    in_specs = (rows, P(("group", "within")), P(), P(), rows, cubes, cubes, rows, rows, rows)
    return jax.shard_map(
        on_device, mesh=mesh, in_specs=in_specs, out_specs=(rows, rows, rows), check_vma=False
    )
```

```python
import functools
import math

import jax
import jax.numpy as jnp
from jax import lax
from jax.experimental import pallas as pl
from jax.experimental.pallas import tpu as pltpu
from jax.sharding import PartitionSpec as P

LEAF = 512
RANK = 64
COLS = 64
ROWS = 4096
NLEAF = 8
ROOT_FIVE = math.sqrt(5.0)
LN_TWO = math.log(2.0)
MESH = pl.DeviceIdType.MESH
FAR = (4, 3, 5, 2, 6, 1, 7)
F32 = jnp.float32
BF16 = jnp.bfloat16
NT = (((1,), (1,)), ((), ()))
NN = (((1,), (0,)), ((), ()))


def split(a):
    high = a.astype(BF16)
    return high, (a - high.astype(F32)).astype(BF16)


def mxu(a, b, dims=NN):
    return lax.dot_general(a, b, dims, preferred_element_type=F32)


def product(a, b, dims=NN):
    ah, al = split(a)
    bh, bl = split(b)
    axis = 1 if dims == NT else 0
    both = mxu(jnp.concatenate([ah, al], axis=1), jnp.concatenate([bh, bh], axis=axis), dims)
    return both + mxu(ah, bl, dims)


def pack(c):
    half = c.shape[0] // 2
    return jnp.concatenate([c[0:half], c[half:]], axis=1)


def unpack(p):
    return jnp.concatenate([p[:, 0:64], p[:, 64:128]], axis=0)


def raise_pair(transfer, left, right):
    return product(
        jnp.concatenate([left, right], axis=1),
        jnp.concatenate([transfer[:, 0:64], transfer[:, 64:128]], axis=0),
    )


def lower(left, transfer, couple, sibling, state):
    if isinstance(left, bool):
        side = transfer[:, 0:64] if left else transfer[:, 64:128]
        across = couple if left else couple.T
    else:
        side = jnp.where(left, transfer[:, 0:64], transfer[:, 64:128])
        across = jnp.where(left, couple, couple.T)
    none = jnp.zeros((64, 64), F32)
    return product(
        jnp.concatenate([jnp.concatenate([sibling, none], axis=0), state], axis=1),
        jnp.concatenate([across, side], axis=1),
        NT,
    )


def identity():
    row = lax.broadcasted_iota(jnp.int32, (128, 64), 0)
    column = lax.broadcasted_iota(jnp.int32, (128, 64), 1)
    return jnp.where(row == column + 64, 1.0, 0.0)


def lower_tree(mats, coefs):
    near = [identity()]
    for height, first in ((3, 12), (2, 8), (1, 0)):
        below = []
        for k, state in enumerate(near):
            t, b = mats(k * 2**height + 2 ** (height - 1) - 1)
            below.append(lower(True, t, b, coefs(first + 2 * k + 1), state))
            below.append(lower(False, t, b, coefs(first + 2 * k), state))
        near = below
    return jnp.concatenate(near, axis=1)


def kernel(
    coords, order, scale, noise, basis, transfer, coupling, res, direc,
    out_image,
    perm, x_in, x_rows, x_perm, b_in, t_in, k_in, r_in, d_in, image,
    d_split, b_split, leaf_c, leaf_f,
    mat_a, mat_z, mat_x, paths, c_a, c_z, c_x, f_top, f_out, pair_c, reduce,
    local_f, local_op, plane_f, plane_op, slab_op, coef,
    in_sem, out_sem, send_sem, rm_a, rm_z, rm_x, r_path, rc_a, rc_z, rc_x, r_f, r_red,
):
    group = lax.axis_index("group")
    within = lax.axis_index("within")
    slab = group
    line = lax.div(within, 8)
    spot = lax.rem(within, 8)
    leader = spot == 7
    top_line = line == 7

    def in_plane(q):
        return (group, line * 8 + q)

    def in_line(q):
        return (group, q * 8 + spot)

    def in_slab(q):
        return (q, within)

    inputs = [
        (transfer, t_in), (coupling, k_in), (direc, d_in), (basis, b_in),
        (coords, x_in), (order, perm), (res, r_in),
    ]
    loads = [
        pltpu.make_async_copy(src, dst, in_sem.at[i]) for i, (src, dst) in enumerate(inputs)
    ]
    for load in loads:
        load.start()

    barrier = pltpu.get_barrier_semaphore()

    def greet(device):
        pl.semaphore_signal(barrier, inc=1, device_id=device, device_id_type=MESH)

    for p in range(1, 8):
        greet(in_plane(lax.rem(spot + p, 8)))
        greet(in_line(lax.rem(line + p, 8)))
    for p in range(1, 4):
        greet(in_slab(lax.rem(slab + p, 4)))

    sends = []

    def remote(src, dst, recv, device):
        index = len(sends)
        copy = pltpu.make_async_remote_copy(
            src_ref=src, dst_ref=dst, send_sem=send_sem.at[index], recv_sem=recv,
            device_id=device, device_id_type=MESH,
        )
        sends.append(copy)
        return copy

    def arrived(dst, recv):
        pltpu.make_async_remote_copy(
            src_ref=dst, dst_ref=dst, send_sem=send_sem.at[0], recv_sem=recv,
            device_id=in_plane(lax.rem(spot + 1, 8)), device_id_type=MESH,
        ).wait_recv()

    loads[0].wait()
    loads[1].wait()
    own = jnp.concatenate([t_in[7], pack(k_in[7])], axis=0)

    @pl.when(jnp.logical_not(leader))
    def _():
        mat_a[spot] = own

    @pl.when(jnp.logical_and(leader, jnp.logical_not(top_line)))
    def _():
        mat_z[line] = own

    @pl.when(jnp.logical_and(leader, top_line))
    def _():
        mat_x[slab] = own

    send_a = [remote(mat_a.at[spot], mat_a.at[spot], rm_a.at[spot], in_plane(7))]
    send_z = [
        remote(mat_z.at[line], mat_z.at[line], rm_z.at[line], in_line(lax.rem(line + p, 8)))
        for p in FAR
    ]
    send_x = [
        remote(mat_x.at[slab], mat_x.at[slab], rm_x.at[slab], in_slab(lax.rem(slab + p, 4)))
        for p in (2, 1, 3)
    ]
    send_p = [remote(paths, paths, r_path, in_line(q)) for q in (3, 4, 2, 5, 1, 6, 0)]

    loads[2].wait()
    loads[3].wait()

    @pl.loop(0, NLEAF)
    def _(leaf):
        at = pl.multiple_of(leaf * LEAF, LEAF)
        dh, dl = split(d_in[:, pl.ds(at, LEAF)])
        bh, bl = split(b_in[:, pl.ds(at, LEAF)])
        both_d = jnp.concatenate([dh, dl], axis=0)
        both_b = jnp.concatenate([bh, bl], axis=0)
        d_split[:, pl.ds(at, LEAF)] = both_d
        b_split[:, pl.ds(at, LEAF)] = both_b
        prod = mxu(both_d, both_b, NT)
        leaf_c[leaf] = (prod[0:64, 0:64] + prod[64:128, 64:128]) + (prod[0:64, 64:128] + prod[64:128, 0:64])

    for k in range(4):
        leaf_c[8 + k] = raise_pair(t_in[2 * k], leaf_c[2 * k], leaf_c[2 * k + 1])
    for k in range(2):
        leaf_c[12 + k] = raise_pair(t_in[4 * k + 1], leaf_c[8 + 2 * k], leaf_c[9 + 2 * k])
    c_a[spot] = pack(raise_pair(t_in[3], leaf_c[12], leaf_c[13]))
    send_ca = [remote(c_a.at[spot], c_a.at[spot], rc_a.at[spot], in_plane(7))]
    owner = jnp.logical_and(jnp.logical_and(leader, top_line), slab < 3)
    pl.semaphore_wait(barrier, 17)
    @pl.when(jnp.logical_not(leader))
    def _():
        for copy in send_ca + send_a:
            copy.start()

    @pl.when(jnp.logical_and(leader, jnp.logical_not(top_line)))
    def _():
        for copy in send_z:
            copy.start()

    @pl.when(owner)
    def _():
        for copy in send_x:
            copy.start()

    loads[4].wait()
    loads[5].wait()

    @pl.loop(0, ROWS // 128)
    def _(i):
        at = pl.multiple_of(i * 128, 128)
        x_rows[pl.ds(at, 128), 0:64] = x_in[:, pl.ds(at, 128)].T * (ROOT_FIVE / LN_TWO * scale[...])

    def gather(at, first, count):
        for j in range(first, first + count):
            x_perm[pl.ds(j, 1), :] = x_rows[pl.ds(perm[at + j], 1), :]

    @pl.loop(0, LEAF // 64)
    def _(i):
        base = pl.multiple_of(i * 64, 64)
        for j in range(64):
            x_perm[pl.ds(base + j, 1), :] = x_rows[pl.ds(perm[base + j], 1), :]

    def dense(first, last):
        @pl.loop(first, last)
        def _(leaf):
            at = pl.multiple_of(leaf * LEAF, LEAF)

            xh, xl = split(x_perm[:, 0:64])
            near = xh.astype(F32) + xl.astype(F32)
            square = jnp.sum(near * near, axis=1, keepdims=True)
            square_row = jnp.broadcast_to(square, (LEAF, 128)).T[0:1]
            minus = jnp.asarray(-2.0, BF16)
            one = jnp.concatenate([xh * minus, xh * minus, xl * minus, xl * minus], axis=1)
            two = jnp.concatenate([xh, xl, xh, xl], axis=1)
            vectors = d_split[:, pl.ds(at, LEAF)]
            following = jnp.minimum(at + LEAF, ROWS - LEAF)
            for c in range(0, LEAF, 256):
                gather(following, c, 256)
                inner = mxu(one, two[c : c + 256], NT)
                dist_sq = jnp.maximum((square + square_row[:, c : c + 256]) + inner, 1e-30)
                dist = dist_sq * lax.rsqrt(dist_sq)
                value = ((1.0 + dist * LN_TWO) + dist_sq * (LN_TWO * LN_TWO / 3.0)) * jnp.exp2(-dist)
                vh, vl = split(value)
                got = mxu(vectors, vh)
                image[:, pl.ds(at + c, 256)] = got[0:64] + (got[64:128] + mxu(vectors[0:64], vl))

    def mats(ref):
        return ref[0:64, :], unpack(ref[64:96, :])

    def mats(ref):
        return ref[0:64, :], unpack(ref[64:96, :])

    dense(0, 0)

    @pl.when(jnp.logical_and(leader, top_line))
    def _():
        for q in range(3):
            @pl.when(slab != q)
            def _():
                arrived(mat_x.at[q], rm_x.at[q])
        half = lax.div(slab, 2)
        side = lax.rem(slab, 2)
        t, b = mats(mat_x.at[half * 2])
        beside = jnp.where(side == 0, b.T, b)
        turn = jnp.where(side == 0, t[:, 0:64], t[:, 64:128])
        t, b = mats(mat_x.at[1])
        across = product(jnp.where(half == 0, b.T, b), turn, NT)
        t, b = mats(mat_x.at[2 - half * 2])
        paths[...] = pack(
            jnp.concatenate([beside, product(t[:, 0:64], across), product(t[:, 64:128], across)], axis=0)
        )
        for copy in send_p:
            copy.start()

    dense(0, 1)

    send_cz = [
        remote(c_z.at[line], c_z.at[line], rc_z.at[line], in_line(lax.rem(line + p, 8)))
        for p in FAR
    ]
    send_cx = [
        remote(c_x.at[slab], c_x.at[slab], rc_x.at[slab], in_slab(lax.rem(slab + p, 4)))
        for p in (2, 1, 3)
    ]
    send_f = [remote(f_out.at[q], f_top, r_f, in_plane(q)) for q in range(7)]

    @pl.when(leader)
    def _():
        for q in range(7):
            arrived(c_a.at[q], rc_a.at[q])
            arrived(mat_a.at[q], rm_a.at[q])
        for k in range(8):
            pair_c[k] = unpack(c_a[k])
        for k in range(4):
            pair_c[8 + k] = raise_pair(mat_a[2 * k, 0:64, :], pair_c[2 * k], pair_c[2 * k + 1])
        for k in range(2):
            pair_c[12 + k] = raise_pair(mat_a[4 * k + 1, 0:64, :], pair_c[8 + 2 * k], pair_c[9 + 2 * k])
        c_z[line] = pack(raise_pair(mat_a[3, 0:64, :], pair_c[12], pair_c[13]))
        for copy in send_cz:
            copy.start()
        plane = lower_tree(lambda i: mats(mat_a.at[i]), lambda i: pair_c[i])
        plane_f[...] = plane[0:64]
        plane_op[...] = plane[64:128]

    dense(1, 4)

    @pl.when(leader)
    def _():
        for p in range(1, 8):
            q = lax.rem(line + p, 8)
            arrived(c_z.at[q], rc_z.at[q])

            @pl.when(q != 7)
            def _():
                arrived(mat_z.at[q], rm_z.at[q])
        for k in range(8):
            pair_c[k] = unpack(c_z[k])
        for k in range(4):
            pair_c[8 + k] = raise_pair(mat_z[2 * k, 0:64, :], pair_c[2 * k], pair_c[2 * k + 1])
        for k in range(2):
            pair_c[12 + k] = raise_pair(mat_z[4 * k + 1, 0:64, :], pair_c[8 + 2 * k], pair_c[9 + 2 * k])
        c_x[slab] = pack(raise_pair(mat_z[3, 0:64, :], pair_c[12], pair_c[13]))
        for copy in send_cx:
            copy.start()

        half = lax.div(line, 4)
        quarter = lax.div(line, 2)
        t, b = mats(mat_z.at[3])
        state = lower(half == 0, t, b, pair_c[13 - half], identity())
        side = lax.rem(quarter, 2)
        t, b = mats(mat_z.at[half * 4 + 1])
        state = lower(side == 0, t, b, pair_c[8 + half * 2 + 1 - side], state)
        side = lax.rem(line, 2)
        t, b = mats(mat_z.at[quarter * 2])
        state = lower(side == 0, t, b, pair_c[quarter * 2 + 1 - side], state)
        both = product(state, plane_op[...])
        plane_f[...] = plane_f[...] + both[0:64]

        @pl.when(jnp.logical_not(top_line))
        def _():
            arrived(paths, r_path)
        slab_op[0], slab_op[1] = split(product(unpack(paths[...]), both[64:128]))

    dense(4, 6)

    @pl.when(leader)
    def _():
        for p in range(1, 4):
            q = lax.rem(slab + p, 4)
            arrived(c_x.at[q], rc_x.at[q])
        half = lax.div(slab, 2)
        others = (half * 2 + 1 - lax.rem(slab, 2), 2 - half * 2, 3 - half * 2)
        ch, cl = split(jnp.concatenate([unpack(c_x[q]) for q in others], axis=1))
        far = plane_f[...] + (mxu(ch, slab_op[0]) + (mxu(ch, slab_op[1]) + mxu(cl, slab_op[0])))
        for q in range(8):
            f_out[q] = pack(far[:, q * 64 : q * 64 + 64])
        for copy in send_f:
            copy.start()
        f_top[...] = f_out[7]

    local = lower_tree(lambda i: (t_in[i], k_in[i]), lambda i: leaf_c[i])
    local_f[...] = local[0:64]
    local_op[0], local_op[1] = split(local[64:128])

    dense(6, 8)

    @pl.when(jnp.logical_not(leader))
    def _():
        arrived(f_top, r_f)
    fh, fl = split(unpack(f_top[...]))
    far = local_f[...] + (mxu(fh, local_op[0]) + (mxu(fh, local_op[1]) + mxu(fl, local_op[0])))
    for k in range(NLEAF):
        fh, fl = split(far[:, k * 64 : k * 64 + 64])
        leaf_f[k] = jnp.concatenate(
            [jnp.concatenate([fh, fh], axis=1), jnp.concatenate([fl, fl], axis=1)], axis=0
        )

    loads[6].wait()
    shift = noise[0]
    zero = jnp.zeros((COLS, 128), F32)

    def store(leaf):
        at = pl.multiple_of(leaf * LEAF, LEAF)
        return pltpu.make_async_copy(
            image.at[:, pl.ds(at, LEAF)], out_image.at[:, pl.ds(at, LEAF)], out_sem.at[leaf]
        )

    def add_leaf(leaf, sums):
        at = pl.multiple_of(leaf * LEAF, LEAF)
        far = mxu(leaf_f[leaf], b_split[:, pl.ds(at, LEAF)])
        d = d_in[:, pl.ds(at, LEAF)]
        r = r_in[:, pl.ds(at, LEAF)]
        q = image[:, pl.ds(at, LEAF)] + shift * d + (far[0:64] + far[64:128])
        image[:, pl.ds(at, LEAF)] = q
        store(leaf).start()
        terms = (r * r, d * q, r * q, q * q)
        return tuple(
            total + ((term[:, 0:128] + term[:, 128:256]) + (term[:, 256:384] + term[:, 384:512]))
            for total, term in zip(sums, terms)
        )

    sums = lax.fori_loop(0, NLEAF, add_leaf, (zero, zero, zero, zero))
    lane = lax.broadcasted_iota(jnp.int32, (COLS, 128), 1)
    table = zero
    for i, total in enumerate(sums):
        table = jnp.where(lane == i, jnp.sum(total, axis=1, keepdims=True), table)
    value = table.T[0:8, :]

    first = 0
    send_red = []
    for size, place, device in ((8, spot, in_plane), (8, line, in_line), (4, slab, in_slab)):
        reduce[first + place, :, 0:64] = value
        copies = []
        for p in FAR if size == 8 else (2, 1, 3):
            q = lax.rem(place + p, size)
            copies.append(
                remote(reduce.at[first + place], reduce.at[first + place], r_red.at[first + place], device(q))
            )
        for copy in copies:
            copy.start()
        send_red.extend(copies)
        for p in range(1, size):
            q = lax.rem(place + p, size)
            arrived(reduce.at[first + q], r_red.at[first + q])
        value = reduce[first, :, 0:64]
        for q in range(1, size):
            value = value + reduce[first + q, :, 0:64]
        first += size

    old, curve, cross, own_square = value[0:1], value[1:2], value[2:3], value[3:4]
    alpha = old / curve
    new = old - 2.0 * alpha * cross + alpha * alpha * own_square
    ratio = new / old
    coef[:, 0:128] = jnp.broadcast_to(alpha, (128, COLS)).T
    coef[:, 128:256] = jnp.broadcast_to(ratio, (128, COLS)).T
    store_coef = pltpu.make_async_copy(coef, out_image.at[:, pl.ds(ROWS, 256)], out_sem.at[NLEAF])
    store_coef.start()

    for copy in send_red:
        copy.wait_send()

    @pl.when(jnp.logical_not(leader))
    def _():
        for copy in send_ca + send_a:
            copy.wait_send()

    @pl.when(leader)
    def _():
        for copy in send_cz + send_cx + send_f:
            copy.wait_send()

    @pl.when(jnp.logical_and(leader, jnp.logical_not(top_line)))
    def _():
        for copy in send_z:
            copy.wait_send()

    @pl.when(owner)
    def _():
        for copy in send_x:
            copy.wait_send()

    @pl.when(jnp.logical_and(leader, top_line))
    def _():
        for copy in send_p:
            copy.wait_send()

    @pl.loop(0, NLEAF)
    def _(leaf):
        store(leaf).wait()

    store_coef.wait()


def finish(image, sol, res, direc, out_sol, out_res, out_dir, held, made, coef, in_sem, out_sem):
    parts = in_sem.shape[1]
    width = ROWS // parts
    load_coef = pltpu.make_async_copy(image.at[:, pl.ds(ROWS, 256)], coef, in_sem.at[4, 0])
    load_coef.start()
    loads = [
        [
            pltpu.make_async_copy(
                src.at[:, pl.ds(k * width, width)], held.at[i, :, pl.ds(k * width, width)], in_sem.at[i, k]
            )
            for i, src in enumerate((image, sol, res, direc))
        ]
        for k in range(parts)
    ]
    stores = [
        [
            pltpu.make_async_copy(
                made.at[i, :, pl.ds(k * width, width)], dst.at[:, pl.ds(k * width, width)], out_sem.at[i, k]
            )
            for i, dst in enumerate((out_sol, out_res, out_dir))
        ]
        for k in range(parts)
    ]
    for part in loads:
        for load in part:
            load.start()
    load_coef.wait()
    alpha = jnp.concatenate([coef[:, 0:128]] * (width // 128), axis=1)
    ratio = jnp.concatenate([coef[:, 128:256]] * (width // 128), axis=1)
    for k in range(parts):
        for load in loads[k]:
            load.wait()
        at = pl.ds(k * width, width)
        d = held[3, :, at]
        r = held[2, :, at] - alpha * held[0, :, at]
        made[0, :, at] = held[1, :, at] + alpha * d
        made[1, :, at] = r
        made[2, :, at] = r + ratio * d
        for store in stores[k]:
            store.start()
    for part in stores:
        for store in part:
            store.wait()


def on_device(
    coords, perm, inv_scale, noise, leaf_basis, pair_transfer, coupling, solution, residual, direction
):
    hbm = pl.BlockSpec(memory_space=pltpu.HBM)
    anywhere = pl.BlockSpec(memory_space=pl.ANY)
    smem = pl.BlockSpec(memory_space=pltpu.SMEM)
    vmem = pl.BlockSpec(memory_space=pltpu.VMEM)
    wide = jax.ShapeDtypeStruct((COLS, ROWS), F32)
    dma = pltpu.SemaphoreType.DMA
    image = pl.pallas_call(
        kernel,
        out_shape=jax.ShapeDtypeStruct((COLS, ROWS + 256), F32),
        in_specs=[hbm, hbm, vmem, smem, hbm, hbm, hbm, hbm, hbm],
        out_specs=anywhere,
        scratch_shapes=[
            pltpu.SMEM((ROWS,), jnp.int32),
            pltpu.VMEM((64, ROWS), F32),
            pltpu.VMEM((ROWS, 128), F32),
            pltpu.VMEM((LEAF, 128), F32),
            pltpu.VMEM((64, ROWS), F32),
            pltpu.VMEM((8, 64, 128), F32),
            pltpu.VMEM((8, 64, 64), F32),
            pltpu.VMEM((64, ROWS), F32),
            pltpu.VMEM((64, ROWS), F32),
            pltpu.VMEM((64, ROWS), F32),
            pltpu.VMEM((128, ROWS), BF16),
            pltpu.VMEM((128, ROWS), BF16),
            pltpu.VMEM((14, 64, 64), F32),
            pltpu.VMEM((8, 128, 128), BF16),
            pltpu.VMEM((8, 96, 128), F32),
            pltpu.VMEM((8, 96, 128), F32),
            pltpu.VMEM((4, 96, 128), F32),
            pltpu.VMEM((96, 128), F32),
            pltpu.VMEM((8, 32, 128), F32),
            pltpu.VMEM((8, 32, 128), F32),
            pltpu.VMEM((4, 32, 128), F32),
            pltpu.VMEM((32, 128), F32),
            pltpu.VMEM((8, 32, 128), F32),
            pltpu.VMEM((14, 64, 64), F32),
            pltpu.VMEM((20, 8, 128), F32),
            pltpu.VMEM((64, LEAF), F32),
            pltpu.VMEM((2, 64, LEAF), BF16),
            pltpu.VMEM((64, LEAF), F32),
            pltpu.VMEM((64, LEAF), F32),
            pltpu.VMEM((2, 192, LEAF), BF16),
            pltpu.VMEM((COLS, 256), F32),
            dma((7,)),
            dma((NLEAF + 1,)),
            dma((96,)),
            dma((8,)),
            dma((8,)),
            dma((4,)),
            dma,
            dma((8,)),
            dma((8,)),
            dma((4,)),
            dma,
            dma((20,)),
        ],
        compiler_params=pltpu.CompilerParams(
            collective_id=0, has_side_effects=True, vmem_limit_bytes=60 * 2**20
        ),
        cost_estimate=pl.CostEstimate(flops=4 * 10**9, bytes_accessed=10 * 2**20, transcendentals=4 * 2**20),
        name="cg_step",
    )(
        coords.T, perm, inv_scale.reshape(1, 64), noise, leaf_basis.T, pair_transfer, coupling,
        residual.T, direction.T,
    )
    parts = 4
    outs = pl.pallas_call(
        finish,
        out_shape=(wide, wide, wide),
        in_specs=[anywhere, anywhere, anywhere, anywhere],
        out_specs=(anywhere, anywhere, anywhere),
        scratch_shapes=[
            pltpu.VMEM((4, COLS, ROWS), F32),
            pltpu.VMEM((3, COLS, ROWS), F32),
            pltpu.VMEM((COLS, 256), F32),
            dma((5, parts)),
            dma((3, parts)),
        ],
        compiler_params=pltpu.CompilerParams(vmem_limit_bytes=12 * 2**20),
        name="cg_finish",
    )(image, solution.T, residual.T, direction.T)
    return tuple(out.T for out in outs)


def solution(mesh):
    rows = P(("group", "within"), None)
    cubes = P(("group", "within"), None, None)
    in_specs = (rows, P(("group", "within")), P(), P(), rows, cubes, cubes, rows, rows, rows)
    return jax.shard_map(
        on_device, mesh=mesh, in_specs=in_specs, out_specs=(rows, rows, rows), check_vma=False
    )
```

```python
import functools
import math

import jax
import jax.numpy as jnp
from jax import lax
from jax.experimental import pallas as pl
from jax.experimental.pallas import tpu as pltpu
from jax.sharding import PartitionSpec as P

LEAF = 512
RANK = 64
COLS = 64
ROWS = 4096
NLEAF = 8
ROOT_FIVE = math.sqrt(5.0)
LN_TWO = math.log(2.0)
MESH = pl.DeviceIdType.MESH
FAR = (4, 3, 5, 2, 6, 1, 7)
F32 = jnp.float32
BF16 = jnp.bfloat16
NT = (((1,), (1,)), ((), ()))
NN = (((1,), (0,)), ((), ()))


def split(a):
    high = a.astype(BF16)
    return high, (a - high.astype(F32)).astype(BF16)


def mxu(a, b, dims=NN):
    return lax.dot_general(a, b, dims, preferred_element_type=F32)


def product(a, b, dims=NN):
    ah, al = split(a)
    bh, bl = split(b)
    axis = 1 if dims == NT else 0
    both = mxu(jnp.concatenate([ah, al], axis=1), jnp.concatenate([bh, bh], axis=axis), dims)
    return both + mxu(ah, bl, dims)


def pack(c):
    half = c.shape[0] // 2
    return jnp.concatenate([c[0:half], c[half:]], axis=1)


def unpack(p):
    return jnp.concatenate([p[:, 0:64], p[:, 64:128]], axis=0)


def raise_pair(transfer, left, right):
    return product(
        jnp.concatenate([left, right], axis=1),
        jnp.concatenate([transfer[:, 0:64], transfer[:, 64:128]], axis=0),
    )


def lower(left, transfer, couple, sibling, state):
    if isinstance(left, bool):
        side = transfer[:, 0:64] if left else transfer[:, 64:128]
        across = couple if left else couple.T
    else:
        side = jnp.where(left, transfer[:, 0:64], transfer[:, 64:128])
        across = jnp.where(left, couple, couple.T)
    none = jnp.zeros((64, 64), F32)
    return product(
        jnp.concatenate([jnp.concatenate([sibling, none], axis=0), state], axis=1),
        jnp.concatenate([across, side], axis=1),
        NT,
    )


def identity():
    row = lax.broadcasted_iota(jnp.int32, (128, 64), 0)
    column = lax.broadcasted_iota(jnp.int32, (128, 64), 1)
    return jnp.where(row == column + 64, 1.0, 0.0)


def lower_tree(mats, coefs):
    near = [identity()]
    for height, first in ((3, 12), (2, 8), (1, 0)):
        below = []
        for k, state in enumerate(near):
            t, b = mats(k * 2**height + 2 ** (height - 1) - 1)
            below.append(lower(True, t, b, coefs(first + 2 * k + 1), state))
            below.append(lower(False, t, b, coefs(first + 2 * k), state))
        near = below
    return jnp.concatenate(near, axis=1)


def kernel(
    coords, order, scale, noise, basis, transfer, coupling, res, direc,
    out_image,
    perm, x_in, x_rows, x_perm, b_in, t_in, k_in, r_in, d_in, image,
    d_split, b_split, leaf_c, leaf_f,
    mat_a, mat_z, mat_x, paths, c_a, c_z, c_x, f_top, f_out, pair_c, reduce,
    local_f, local_op, plane_f, plane_op, slab_op, coef,
    in_sem, out_sem, send_sem, rm_a, rm_z, rm_x, r_path, rc_a, rc_z, rc_x, r_f, r_red,
):
    group = lax.axis_index("group")
    within = lax.axis_index("within")
    slab = group
    line = lax.div(within, 8)
    spot = lax.rem(within, 8)
    leader = spot == 7
    top_line = line == 7

    def in_plane(q):
        return (group, line * 8 + q)

    def in_line(q):
        return (group, q * 8 + spot)

    def in_slab(q):
        return (q, within)

    inputs = [
        (transfer, t_in), (coupling, k_in), (direc, d_in), (basis, b_in),
        (coords, x_in), (order, perm), (res, r_in),
    ]
    loads = [
        pltpu.make_async_copy(src, dst, in_sem.at[i]) for i, (src, dst) in enumerate(inputs)
    ]
    for load in loads:
        load.start()

    barrier = pltpu.get_barrier_semaphore()

    def greet(device):
        pl.semaphore_signal(barrier, inc=1, device_id=device, device_id_type=MESH)

    for p in range(1, 8):
        greet(in_plane(lax.rem(spot + p, 8)))
        greet(in_line(lax.rem(line + p, 8)))
    for p in range(1, 4):
        greet(in_slab(lax.rem(slab + p, 4)))

    sends = []

    def remote(src, dst, recv, device):
        index = len(sends)
        copy = pltpu.make_async_remote_copy(
            src_ref=src, dst_ref=dst, send_sem=send_sem.at[index], recv_sem=recv,
            device_id=device, device_id_type=MESH,
        )
        sends.append(copy)
        return copy

    def arrived(dst, recv):
        pltpu.make_async_remote_copy(
            src_ref=dst, dst_ref=dst, send_sem=send_sem.at[0], recv_sem=recv,
            device_id=in_plane(lax.rem(spot + 1, 8)), device_id_type=MESH,
        ).wait_recv()

    loads[0].wait()
    loads[1].wait()
    own = jnp.concatenate([t_in[7], pack(k_in[7])], axis=0)

    @pl.when(jnp.logical_not(leader))
    def _():
        mat_a[spot] = own

    @pl.when(jnp.logical_and(leader, jnp.logical_not(top_line)))
    def _():
        mat_z[line] = own

    @pl.when(jnp.logical_and(leader, top_line))
    def _():
        mat_x[slab] = own

    send_a = [remote(mat_a.at[spot], mat_a.at[spot], rm_a.at[spot], in_plane(7))]
    send_z = [
        remote(mat_z.at[line], mat_z.at[line], rm_z.at[line], in_line(lax.rem(line + p, 8)))
        for p in FAR
    ]
    send_x = [
        remote(mat_x.at[slab], mat_x.at[slab], rm_x.at[slab], in_slab(lax.rem(slab + p, 4)))
        for p in (2, 1, 3)
    ]
    send_p = [remote(paths, paths, r_path, in_line(q)) for q in (3, 4, 2, 5, 1, 6, 0)]

    loads[2].wait()
    loads[3].wait()

    @pl.loop(0, NLEAF)
    def _(leaf):
        at = pl.multiple_of(leaf * LEAF, LEAF)
        dh, dl = split(d_in[:, pl.ds(at, LEAF)])
        bh, bl = split(b_in[:, pl.ds(at, LEAF)])
        both_d = jnp.concatenate([dh, dl], axis=0)
        both_b = jnp.concatenate([bh, bl], axis=0)
        d_split[:, pl.ds(at, LEAF)] = both_d
        b_split[:, pl.ds(at, LEAF)] = both_b
        prod = mxu(both_d, both_b, NT)
        leaf_c[leaf] = (prod[0:64, 0:64] + prod[64:128, 64:128]) + (prod[0:64, 64:128] + prod[64:128, 0:64])

    for k in range(4):
        leaf_c[8 + k] = raise_pair(t_in[2 * k], leaf_c[2 * k], leaf_c[2 * k + 1])
    for k in range(2):
        leaf_c[12 + k] = raise_pair(t_in[4 * k + 1], leaf_c[8 + 2 * k], leaf_c[9 + 2 * k])
    c_a[spot] = pack(raise_pair(t_in[3], leaf_c[12], leaf_c[13]))
    send_ca = [remote(c_a.at[spot], c_a.at[spot], rc_a.at[spot], in_plane(7))]
    owner = jnp.logical_and(jnp.logical_and(leader, top_line), slab < 3)
    pl.semaphore_wait(barrier, 17)
    @pl.when(jnp.logical_not(leader))
    def _():
        for copy in send_ca + send_a:
            copy.start()

    @pl.when(jnp.logical_and(leader, jnp.logical_not(top_line)))
    def _():
        for copy in send_z:
            copy.start()

    @pl.when(owner)
    def _():
        for copy in send_x:
            copy.start()

    loads[4].wait()
    loads[5].wait()

    @pl.loop(0, ROWS // 128)
    def _(i):
        at = pl.multiple_of(i * 128, 128)
        x_rows[pl.ds(at, 128), 0:64] = x_in[:, pl.ds(at, 128)].T * (ROOT_FIVE / LN_TWO * scale[...])

    def gather(at, first, count):
        for j in range(first, first + count):
            x_perm[pl.ds(j, 1), :] = x_rows[pl.ds(perm[at + j], 1), :]

    @pl.loop(0, LEAF // 64)
    def _(i):
        base = pl.multiple_of(i * 64, 64)
        for j in range(64):
            x_perm[pl.ds(base + j, 1), :] = x_rows[pl.ds(perm[base + j], 1), :]

    def dense(first, last):
        @pl.loop(first, last)
        def _(leaf):
            at = pl.multiple_of(leaf * LEAF, LEAF)

            xh, xl = split(x_perm[:, 0:64])
            near = xh.astype(F32) + xl.astype(F32)
            square = jnp.sum(near * near, axis=1, keepdims=True)
            square_row = jnp.broadcast_to(square, (LEAF, 128)).T[0:1]
            minus = jnp.asarray(-2.0, BF16)
            one = jnp.concatenate([xh * minus, xh * minus, xl * minus, xl * minus], axis=1)
            two = jnp.concatenate([xh, xl, xh, xl], axis=1)
            vectors = d_split[:, pl.ds(at, LEAF)]
            following = jnp.minimum(at + LEAF, ROWS - LEAF)
            for c in range(0, LEAF, 256):
                gather(following, c, 256)
                inner = mxu(one, two[c : c + 256], NT)
                dist_sq = jnp.maximum((square + square_row[:, c : c + 256]) + inner, 1e-30)
                dist = dist_sq * lax.rsqrt(dist_sq)
                value = ((1.0 + dist * LN_TWO) + dist_sq * (LN_TWO * LN_TWO / 3.0)) * jnp.exp2(-dist)
                vh, vl = split(value)
                got = mxu(vectors, vh)
                image[:, pl.ds(at + c, 256)] = got[0:64] + (got[64:128] + mxu(vectors[0:64], vl))

    def mats(ref):
        return ref[0:64, :], unpack(ref[64:96, :])

    def mats(ref):
        return ref[0:64, :], unpack(ref[64:96, :])

    dense(0, 0)

    @pl.when(jnp.logical_and(leader, top_line))
    def _():
        for q in range(3):
            @pl.when(slab != q)
            def _():
                arrived(mat_x.at[q], rm_x.at[q])
        half = lax.div(slab, 2)
        side = lax.rem(slab, 2)
        t, b = mats(mat_x.at[half * 2])
        beside = jnp.where(side == 0, b.T, b)
        turn = jnp.where(side == 0, t[:, 0:64], t[:, 64:128])
        t, b = mats(mat_x.at[1])
        across = product(jnp.where(half == 0, b.T, b), turn, NT)
        t, b = mats(mat_x.at[2 - half * 2])
        paths[...] = pack(
            jnp.concatenate([beside, product(t[:, 0:64], across), product(t[:, 64:128], across)], axis=0)
        )
        for copy in send_p:
            copy.start()

    dense(0, 1)

    send_cz = [
        remote(c_z.at[line], c_z.at[line], rc_z.at[line], in_line(lax.rem(line + p, 8)))
        for p in FAR
    ]
    send_cx = [
        remote(c_x.at[slab], c_x.at[slab], rc_x.at[slab], in_slab(lax.rem(slab + p, 4)))
        for p in (2, 1, 3)
    ]
    send_f = [remote(f_out.at[q], f_top, r_f, in_plane(q)) for q in range(7)]

    @pl.when(leader)
    def _():
        for q in range(7):
            arrived(c_a.at[q], rc_a.at[q])
            arrived(mat_a.at[q], rm_a.at[q])
        for k in range(8):
            pair_c[k] = unpack(c_a[k])
        for k in range(4):
            pair_c[8 + k] = raise_pair(mat_a[2 * k, 0:64, :], pair_c[2 * k], pair_c[2 * k + 1])
        for k in range(2):
            pair_c[12 + k] = raise_pair(mat_a[4 * k + 1, 0:64, :], pair_c[8 + 2 * k], pair_c[9 + 2 * k])
        c_z[line] = pack(raise_pair(mat_a[3, 0:64, :], pair_c[12], pair_c[13]))
        for copy in send_cz:
            copy.start()
        plane = lower_tree(lambda i: mats(mat_a.at[i]), lambda i: pair_c[i])
        plane_f[...] = plane[0:64]
        plane_op[...] = plane[64:128]

    dense(1, 4)

    @pl.when(leader)
    def _():
        for p in range(1, 8):
            q = lax.rem(line + p, 8)
            arrived(c_z.at[q], rc_z.at[q])

            @pl.when(q != 7)
            def _():
                arrived(mat_z.at[q], rm_z.at[q])
        for k in range(8):
            pair_c[k] = unpack(c_z[k])
        for k in range(4):
            pair_c[8 + k] = raise_pair(mat_z[2 * k, 0:64, :], pair_c[2 * k], pair_c[2 * k + 1])
        for k in range(2):
            pair_c[12 + k] = raise_pair(mat_z[4 * k + 1, 0:64, :], pair_c[8 + 2 * k], pair_c[9 + 2 * k])
        c_x[slab] = pack(raise_pair(mat_z[3, 0:64, :], pair_c[12], pair_c[13]))
        for copy in send_cx:
            copy.start()

        half = lax.div(line, 4)
        quarter = lax.div(line, 2)
        t, b = mats(mat_z.at[3])
        state = lower(half == 0, t, b, pair_c[13 - half], identity())
        side = lax.rem(quarter, 2)
        t, b = mats(mat_z.at[half * 4 + 1])
        state = lower(side == 0, t, b, pair_c[8 + half * 2 + 1 - side], state)
        side = lax.rem(line, 2)
        t, b = mats(mat_z.at[quarter * 2])
        state = lower(side == 0, t, b, pair_c[quarter * 2 + 1 - side], state)
        both = product(state, plane_op[...])
        plane_f[...] = plane_f[...] + both[0:64]

        @pl.when(jnp.logical_not(top_line))
        def _():
            arrived(paths, r_path)
        slab_op[0], slab_op[1] = split(product(unpack(paths[...]), both[64:128]))

    dense(4, 6)

    @pl.when(leader)
    def _():
        for p in range(1, 4):
            q = lax.rem(slab + p, 4)
            arrived(c_x.at[q], rc_x.at[q])
        half = lax.div(slab, 2)
        others = (half * 2 + 1 - lax.rem(slab, 2), 2 - half * 2, 3 - half * 2)
        ch, cl = split(jnp.concatenate([unpack(c_x[q]) for q in others], axis=1))
        far = plane_f[...] + (mxu(ch, slab_op[0]) + (mxu(ch, slab_op[1]) + mxu(cl, slab_op[0])))
        for q in range(8):
            f_out[q] = pack(far[:, q * 64 : q * 64 + 64])
        for copy in send_f:
            copy.start()
        f_top[...] = f_out[7]

    local = lower_tree(lambda i: (t_in[i], k_in[i]), lambda i: leaf_c[i])
    local_f[...] = local[0:64]
    local_op[0], local_op[1] = split(local[64:128])

    dense(6, 8)

    @pl.when(jnp.logical_not(leader))
    def _():
        arrived(f_top, r_f)
    fh, fl = split(unpack(f_top[...]))
    far = local_f[...] + (mxu(fh, local_op[0]) + (mxu(fh, local_op[1]) + mxu(fl, local_op[0])))
    for k in range(NLEAF):
        fh, fl = split(far[:, k * 64 : k * 64 + 64])
        leaf_f[k] = jnp.concatenate(
            [jnp.concatenate([fh, fh], axis=1), jnp.concatenate([fl, fl], axis=1)], axis=0
        )

    loads[6].wait()
    shift = noise[0]
    zero = jnp.zeros((COLS, 128), F32)

    def store(leaf):
        at = pl.multiple_of(leaf * LEAF, LEAF)
        return pltpu.make_async_copy(
            image.at[:, pl.ds(at, LEAF)], out_image.at[:, pl.ds(at, LEAF)], out_sem.at[leaf]
        )

    def add_leaf(leaf, sums):
        at = pl.multiple_of(leaf * LEAF, LEAF)
        far = mxu(leaf_f[leaf], b_split[:, pl.ds(at, LEAF)])
        d = d_in[:, pl.ds(at, LEAF)]
        r = r_in[:, pl.ds(at, LEAF)]
        q = image[:, pl.ds(at, LEAF)] + shift * d + (far[0:64] + far[64:128])
        image[:, pl.ds(at, LEAF)] = q
        store(leaf).start()
        terms = (r * r, d * q, r * q, q * q)
        return tuple(
            total + ((term[:, 0:128] + term[:, 128:256]) + (term[:, 256:384] + term[:, 384:512]))
            for total, term in zip(sums, terms)
        )

    sums = lax.fori_loop(0, NLEAF, add_leaf, (zero, zero, zero, zero))
    lane = lax.broadcasted_iota(jnp.int32, (COLS, 128), 1)
    table = zero
    for i, total in enumerate(sums):
        table = jnp.where(lane == i, jnp.sum(total, axis=1, keepdims=True), table)
    value = table.T[0:8, :]

    first = 0
    send_red = []
    for size, place, device in ((8, spot, in_plane), (8, line, in_line), (4, slab, in_slab)):
        reduce[first + place, :, 0:64] = value
        copies = []
        for p in FAR if size == 8 else (2, 1, 3):
            q = lax.rem(place + p, size)
            copies.append(
                remote(reduce.at[first + place], reduce.at[first + place], r_red.at[first + place], device(q))
            )
        for copy in copies:
            copy.start()
        send_red.extend(copies)
        for p in range(1, size):
            q = lax.rem(place + p, size)
            arrived(reduce.at[first + q], r_red.at[first + q])
        value = reduce[first, :, 0:64]
        for q in range(1, size):
            value = value + reduce[first + q, :, 0:64]
        first += size

    old, curve, cross, own_square = value[0:1], value[1:2], value[2:3], value[3:4]
    alpha = old / curve
    new = old - 2.0 * alpha * cross + alpha * alpha * own_square
    ratio = new / old
    coef[:, 0:128] = jnp.broadcast_to(alpha, (128, COLS)).T
    coef[:, 128:256] = jnp.broadcast_to(ratio, (128, COLS)).T
    store_coef = pltpu.make_async_copy(coef, out_image.at[:, pl.ds(ROWS, 256)], out_sem.at[NLEAF])
    store_coef.start()

    for copy in send_red:
        copy.wait_send()

    @pl.when(jnp.logical_not(leader))
    def _():
        for copy in send_ca + send_a:
            copy.wait_send()

    @pl.when(leader)
    def _():
        for copy in send_cz + send_cx + send_f:
            copy.wait_send()

    @pl.when(jnp.logical_and(leader, jnp.logical_not(top_line)))
    def _():
        for copy in send_z:
            copy.wait_send()

    @pl.when(owner)
    def _():
        for copy in send_x:
            copy.wait_send()

    @pl.when(jnp.logical_and(leader, top_line))
    def _():
        for copy in send_p:
            copy.wait_send()

    @pl.loop(0, NLEAF)
    def _(leaf):
        store(leaf).wait()

    store_coef.wait()


def finish(image, sol, res, direc, out_sol, out_res, out_dir, made, out_sem):
    parts = out_sem.shape[1]
    width = ROWS // parts
    alpha = jnp.concatenate([image[:, ROWS : ROWS + 128]] * (width // 128), axis=1)
    ratio = jnp.concatenate([image[:, ROWS + 128 : ROWS + 256]] * (width // 128), axis=1)
    stores = []
    for k in range(parts):
        at = pl.ds(k * width, width)
        d = direc[:, at]
        r = res[:, at] - alpha * image[:, at]
        made[0, :, at] = sol[:, at] + alpha * d
        made[1, :, at] = r
        made[2, :, at] = r + ratio * d
        for i, dst in enumerate((out_sol, out_res, out_dir)):
            store = pltpu.make_async_copy(made.at[i, :, at], dst.at[:, at], out_sem.at[i, k])
            store.start()
            stores.append(store)
    for store in stores:
        store.wait()


def on_device(
    coords, perm, inv_scale, noise, leaf_basis, pair_transfer, coupling, solution, residual, direction
):
    hbm = pl.BlockSpec(memory_space=pltpu.HBM)
    anywhere = pl.BlockSpec(memory_space=pl.ANY)
    smem = pl.BlockSpec(memory_space=pltpu.SMEM)
    vmem = pl.BlockSpec(memory_space=pltpu.VMEM)
    wide = jax.ShapeDtypeStruct((COLS, ROWS), F32)
    dma = pltpu.SemaphoreType.DMA
    image = pl.pallas_call(
        kernel,
        out_shape=jax.ShapeDtypeStruct((COLS, ROWS + 256), F32),
        in_specs=[hbm, hbm, vmem, smem, hbm, hbm, hbm, hbm, hbm],
        out_specs=anywhere,
        scratch_shapes=[
            pltpu.SMEM((ROWS,), jnp.int32),
            pltpu.VMEM((64, ROWS), F32),
            pltpu.VMEM((ROWS, 128), F32),
            pltpu.VMEM((LEAF, 128), F32),
            pltpu.VMEM((64, ROWS), F32),
            pltpu.VMEM((8, 64, 128), F32),
            pltpu.VMEM((8, 64, 64), F32),
            pltpu.VMEM((64, ROWS), F32),
            pltpu.VMEM((64, ROWS), F32),
            pltpu.VMEM((64, ROWS), F32),
            pltpu.VMEM((128, ROWS), BF16),
            pltpu.VMEM((128, ROWS), BF16),
            pltpu.VMEM((14, 64, 64), F32),
            pltpu.VMEM((8, 128, 128), BF16),
            pltpu.VMEM((8, 96, 128), F32),
            pltpu.VMEM((8, 96, 128), F32),
            pltpu.VMEM((4, 96, 128), F32),
            pltpu.VMEM((96, 128), F32),
            pltpu.VMEM((8, 32, 128), F32),
            pltpu.VMEM((8, 32, 128), F32),
            pltpu.VMEM((4, 32, 128), F32),
            pltpu.VMEM((32, 128), F32),
            pltpu.VMEM((8, 32, 128), F32),
            pltpu.VMEM((14, 64, 64), F32),
            pltpu.VMEM((20, 8, 128), F32),
            pltpu.VMEM((64, LEAF), F32),
            pltpu.VMEM((2, 64, LEAF), BF16),
            pltpu.VMEM((64, LEAF), F32),
            pltpu.VMEM((64, LEAF), F32),
            pltpu.VMEM((2, 192, LEAF), BF16),
            pltpu.VMEM((COLS, 256), F32),
            dma((7,)),
            dma((NLEAF + 1,)),
            dma((96,)),
            dma((8,)),
            dma((8,)),
            dma((4,)),
            dma,
            dma((8,)),
            dma((8,)),
            dma((4,)),
            dma,
            dma((20,)),
        ],
        compiler_params=pltpu.CompilerParams(
            collective_id=0, has_side_effects=True, vmem_limit_bytes=60 * 2**20
        ),
        cost_estimate=pl.CostEstimate(flops=4 * 10**9, bytes_accessed=10 * 2**20, transcendentals=4 * 2**20),
        name="cg_step",
    )(
        coords.T, perm, inv_scale.reshape(1, 64), noise, leaf_basis.T, pair_transfer, coupling,
        residual.T, direction.T,
    )
    parts = 4
    outs = pl.pallas_call(
        finish,
        out_shape=(wide, wide, wide),
        in_specs=[vmem, vmem, vmem, vmem],
        out_specs=(anywhere, anywhere, anywhere),
        scratch_shapes=[
            pltpu.VMEM((3, COLS, ROWS), F32),
            dma((3, parts)),
        ],
        compiler_params=pltpu.CompilerParams(vmem_limit_bytes=12 * 2**20),
        name="cg_finish",
    )(image, solution.T, residual.T, direction.T)
    return tuple(out.T for out in outs)


def solution(mesh):
    rows = P(("group", "within"), None)
    cubes = P(("group", "within"), None, None)
    in_specs = (rows, P(("group", "within")), P(), P(), rows, cubes, cubes, rows, rows, rows)
    return jax.shard_map(
        on_device, mesh=mesh, in_specs=in_specs, out_specs=(rows, rows, rows), check_vma=False
    )
```
